32 devices in a mesh: dev: 8 (over z, x), rep: 4 (over y, core).
Axes of the slice: x: 2, y: 2, z: 4, core: 2. Of those that a mesh axis runs over, the one named last changes fastest.
Arguments:
- activations: bfloat16 [4, 64, 64, 512], P('rep', 'dev'), may hold values from -6 to 6
- out_grads: bfloat16 [4, 64, 64, 256], P('rep', 'dev'), may hold values from -6 to 6
- inverse: float32 [8, 2048, 2048], P('dev'), may hold values from -4 to 11, as said below
Outputs:
- whitened: float32 [4, 64, 16384], P('rep', 'dev')
- leverage: float32 [4, 64], P('rep', 'dev')
- new_inverse: float32 [8, 2048, 2048], P('dev', 'rep')
The draws below stay inside these ranges and needn't reach their ends.
Inputs may be any that keep to these rules, and one draw needn't show every extreme that they name: Each 2048 x 2048 matrix of inverse is symmetric positive definite.
All inputs are finite; a program needn't handle non-finite values.
Results may differ from the reference program's by a relative error of at most 0.0003.
Values sent between devices are 32-bit elements; how exact they have to be, the bound alone decides.
A program may use at most 128 MiB of HBM per device.

```python
import jax
import jax.numpy as jnp
from jax import lax

KI = 64
KO = 32
KF = 2048
TOK = 64
MODS = 8
GROUP = 64
GROUPS = 4


def draw_inverse(key, part):
    first_key, second_key = jax.random.split(jax.random.fold_in(key, 17))
    growth = jnp.exp(jnp.log(3.0) * jnp.arange(MODS, dtype=jnp.float32) / max(MODS - 1, 1))
    factor = jax.random.uniform(second_key, (MODS,), jnp.float32, 1.0, 1.5)
    unit = jnp.clip(jax.random.normal(first_key, (MODS, KF, KF), jnp.float32), -5.0, 5.0)
    gaussian = unit * (0.35 / KF ** 0.5)
    symmetric = (gaussian + jnp.swapaxes(gaussian, 1, 2)) / 2.0 ** 0.5
    module_scale = growth * factor
    return (module_scale[:, None, None] * (jnp.eye(KF, dtype=jnp.float32)[None] + symmetric)).astype(jnp.float32)


def steps_of(own_key, dims, cuts, low, top_value):
    gain = 1.0
    for axis_at, parts in cuts:
        steps = jax.random.uniform(jax.random.fold_in(jax.random.fold_in(own_key, 6), axis_at), (parts,), jnp.float32, low / len(cuts), top_value / len(cuts))
        gain = gain * jnp.repeat(jnp.exp(steps), dims[axis_at] // parts).reshape((-1,) + (1,) * (len(dims) - 1 - axis_at))
    return gain


def scatter_about(rng, dims, spread, most, cuts=(), kind=jnp.bfloat16):
    loudness = steps_of(rng, dims, cuts, -0.22, 0.18) if cuts else 1.0
    values = jax.random.normal(rng, dims, jnp.float32) * spread * loudness
    return jnp.minimum(jnp.maximum(values, -most), most).astype(kind)


def setup_inputs(seed: int = 0) -> dict:
    streams_of = jax.random.split(jax.random.key(seed), 4)
    activations = scatter_about(streams_of[0], (GROUPS, GROUP, TOK, MODS * KI), 1.0, 6.0, ((0, 4), (1, 8)))
    out_grads = scatter_about(streams_of[1], (GROUPS, GROUP, TOK, MODS * KO), 1.0, 6.0, ((0, 4), (1, 8)))
    inverse = draw_inverse(jax.random.fold_in(streams_of[3], 71), 0)
    return {"activations": activations, "out_grads": out_grads, "inverse": inverse}


def reference(activations, out_grads, inverse):
    total = GROUPS * GROUP
    acts_f = activations.reshape(total, TOK, MODS, KI).astype(jnp.float32)
    grads_f = out_grads.reshape(total, TOK, MODS, KO).astype(jnp.float32)
    features = jnp.einsum('ntmo,ntmi->mnoi', grads_f, acts_f, precision=lax.Precision.HIGHEST)
    features = features.reshape(MODS, total, KF) * TOK ** (-0.5)
    white = jnp.einsum('mnk,mkl->mnl', features, inverse, precision=lax.Precision.HIGHEST)
    leverage = jnp.sum(features * white, axis=(0, 2)) / (MODS * KF)
    damping = 1.0 + KF * leverage

    def update(packed):
        rows_m, white_m, inverse_m = packed
        capacitance = jnp.dot(rows_m, white_m.T, precision=lax.Precision.HIGHEST) + jnp.diag(damping)
        factor = jnp.linalg.cholesky(capacitance)
        solved = jax.scipy.linalg.cho_solve((factor, True), white_m)
        return inverse_m - jnp.dot(white_m.T, solved, precision=lax.Precision.HIGHEST)
    new_inverse = lax.map(update, (features, white, inverse))
    whitened = white.transpose(1, 0, 2).reshape(GROUPS, GROUP, MODS * KF)
    return (whitened, leverage.reshape(GROUPS, GROUP), new_inverse)
```

```python
import functools

import jax
import jax.numpy as jnp
from jax import lax
from jax.experimental import pallas as pl
from jax.experimental.pallas import tpu as pltpu
from jax.sharding import PartitionSpec as P

KI = 64
KO = 32
VMEM_BYTES = 58 * 1024 * 1024
BLOCK = 128
PANEL = 32


def two_terms(value):
    high = value.astype(jnp.bfloat16)
    low = (value - high.astype(jnp.float32)).astype(jnp.bfloat16)
    return high, low


def dot3(left, right, dims):
    left_high, left_low = left
    right_high, right_low = right
    dot = functools.partial(
        lax.dot_general,
        dimension_numbers=(dims, ((), ())),
        preferred_element_type=jnp.float32,
    )
    return dot(left_high, right_high) + (dot(left_high, right_low) + dot(left_low, right_high))


def dot_full(left, right):
    return jnp.dot(
        left, right, precision=lax.Precision.HIGHEST, preferred_element_type=jnp.float32
    )


def gather_kernel(
    num_dev,
    num_rep,
    examples,
    send_ref,
    inverse_ref,
    white_ref,
    cap_ref,
    lev_ref,
    rows,
    columns,
    cols_high,
    cols_low,
    lev_dev,
    lev_rep,
    load_sem,
    own_sem,
    a2a_send,
    a2a_recv,
    row_send,
    row_recv,
    white_send,
    white_recv,
    lev_send,
    lev_recv,
    lrep_send,
    lrep_recv,
):
    dev = lax.axis_index("dev")
    rep = lax.axis_index("rep")
    group = num_dev * examples
    total = num_rep * group
    width = columns.shape[1]
    low_count = 2 if num_rep % 2 == 0 else 1
    high_count = num_rep // low_count
    low = lax.rem(rep, low_count)
    high = rep // low_count
    sibling = high * low_count + (low_count - 1 - low)

    def high_peer(step):
        return lax.rem(high + step, high_count) * low_count + low

    def high_source(step):
        return lax.rem(high + high_count - step, high_count) * low_count + low

    load = pltpu.make_async_copy(
        inverse_ref.at[0, :, pl.ds(pl.multiple_of(rep * width, 128), width)], columns, load_sem
    )
    load.start()

    barrier = pltpu.get_barrier_semaphore()
    for step in range(1, num_dev):
        pl.semaphore_signal(
            barrier, inc=1, device_id={"dev": lax.rem(dev + step, num_dev), "rep": rep}
        )
    for step in range(1, num_rep):
        pl.semaphore_signal(
            barrier, inc=1, device_id={"dev": dev, "rep": lax.rem(rep + step, num_rep)}
        )
    pl.semaphore_wait(barrier, num_dev - 1 + num_rep - 1)

    def row_slice(owner_rep, source):
        return rows.at[pl.ds(pl.multiple_of(owner_rep * group + source * examples, 8), examples)]

    def a2a(step):
        target = lax.rem(dev + step, num_dev)
        return pltpu.make_async_remote_copy(
            src_ref=send_ref.at[target],
            dst_ref=row_slice(rep, dev),
            send_sem=a2a_send.at[step],
            recv_sem=a2a_recv.at[step],
            device_id={"dev": target, "rep": rep},
        )

    own = pltpu.make_async_copy(send_ref.at[dev], row_slice(rep, dev), own_sem)
    own.start()

    def start_a2a(step, carry):
        a2a(step).start()
        return carry

    lax.fori_loop(1, num_dev, start_a2a, 0)

    def pass_on(owner, source, kind, slot, target):
        piece = row_slice(owner, source)
        return pltpu.make_async_remote_copy(
            src_ref=piece,
            dst_ref=piece,
            send_sem=row_send.at[kind, slot],
            recv_sem=row_recv.at[kind, slot],
            device_id={"dev": dev, "rep": target},
        )

    def source_at(step):
        return lax.rem(dev + num_dev - step, num_dev)

    def send_on(step):
        source = source_at(step)
        for far in range(1, high_count):
            pass_on(rep, source, far, step, high_peer(far)).start()
        if low_count == 2:
            pass_on(rep, source, 0, step, sibling).start()

    own.wait()
    send_on(0)
    load.wait()
    high_part, low_part = two_terms(columns[...])
    cols_high[...] = high_part
    cols_low[...] = low_part

    def on_arrival(step, carry):
        a2a(step).wait_recv()
        send_on(step)
        return carry

    lax.fori_loop(1, num_dev, on_arrival, 0)

    def forward(step, carry):
        for far in range(1, high_count):
            pass_on(high_source(far), source_at(step), far, step, rep).wait_recv()
            if low_count == 2:
                pass_on(
                    high_source(far), source_at(step), high_count + far, step, sibling
                ).start()
        return carry

    lax.fori_loop(0, num_dev, forward, 0)

    def finish(step, carry):
        if low_count == 2:
            pass_on(sibling, source_at(step), 0, step, rep).wait_recv()
            for far in range(1, high_count):
                pass_on(sibling, source_at(step), high_count + far, step, rep).wait_recv()
        return carry

    lax.fori_loop(0, num_dev, finish, 0)

    tile = min(256, total)
    own_white = white_ref.at[rep]

    def white_tile(at, carry):
        where = pl.ds(pl.multiple_of(at * tile, tile), tile)
        own_white[where, :] = dot3(
            two_terms(rows[where, :]), (cols_high[...], cols_low[...]), ((1,), (0,))
        )
        return carry

    lax.fori_loop(0, total // tile, white_tile, 0)

    def white_on(owner, part, kind, target):
        piece = white_ref.at[owner, pl.ds(part * group, group)]
        return pltpu.make_async_remote_copy(
            src_ref=piece,
            dst_ref=piece,
            send_sem=white_send.at[kind, part],
            recv_sem=white_recv.at[kind, part],
            device_id={"dev": dev, "rep": target},
        )

    for part in range(num_rep):
        for far in range(1, high_count):
            white_on(rep, part, far, high_peer(far)).start()
        if low_count == 2:
            white_on(rep, part, 0, sibling).start()

    def add_capacitance(block):
        row_block = two_terms(
            rows[:, pl.ds(pl.multiple_of(block * width, 128), width)]
        )
        return dot3(row_block, two_terms(white_ref[block]), ((1,), (1,)))

    diagonal = lax.broadcasted_iota(jnp.int32, (total, total), 0) == lax.broadcasted_iota(
        jnp.int32, (total, total), 1
    )
    cap_ref[...] = add_capacitance(rep)
    own_terms = jnp.sum(jnp.where(diagonal, cap_ref[...], 0.0), axis=0, keepdims=True)
    lev_dev[0] = jnp.broadcast_to(own_terms, (8, total))

    def lev_copy(step):
        return pltpu.make_async_remote_copy(
            src_ref=lev_dev.at[0],
            dst_ref=lev_dev.at[step],
            send_sem=lev_send.at[step],
            recv_sem=lev_recv.at[step],
            device_id={"dev": lax.rem(dev + step, num_dev), "rep": rep},
        )

    def lev_start(step, carry):
        lev_copy(step).start()
        return carry

    lax.fori_loop(1, num_dev, lev_start, 0)

    def lev_wait(step, carry):
        lev_copy(step).wait_recv()
        return carry

    lax.fori_loop(1, num_dev, lev_wait, 0)
    lev_rep[0] = jnp.sum(lev_dev[...], axis=0)

    def lrep_copy(step):
        return pltpu.make_async_remote_copy(
            src_ref=lev_rep.at[0],
            dst_ref=lev_rep.at[step],
            send_sem=lrep_send.at[step],
            recv_sem=lrep_recv.at[step],
            device_id={"dev": dev, "rep": lax.rem(rep + step, num_rep)},
        )

    for step in range(1, num_rep):
        lrep_copy(step).start()

    if low_count == 2:
        for part in range(num_rep):
            white_on(sibling, part, 0, rep).wait_recv()
        cap_ref[...] += add_capacitance(sibling)
    for far in range(1, high_count):
        source = high_source(far)
        for part in range(num_rep):
            white_on(source, part, far, rep).wait_recv()
            if low_count == 2:
                white_on(source, part, high_count + far, sibling).start()
        cap_ref[...] += add_capacitance(source)
    if low_count == 2:
        for far in range(1, high_count):
            source = lax.rem(high + high_count - far, high_count) * 2 + (1 - low)
            for part in range(num_rep):
                white_on(source, part, high_count + far, rep).wait_recv()
            cap_ref[...] += add_capacitance(source)

    for step in range(1, num_rep):
        lrep_copy(step).wait_recv()
    leverage = jnp.sum(lev_rep[...], axis=0) / (num_dev * width * num_rep)
    lev_ref[...] = leverage
    damping = 1.0 + (width * num_rep) * leverage[0:1, :]
    cap_ref[...] = cap_ref[...] + jnp.where(diagonal, damping, 0.0)

    def drain(step, carry):
        a2a(step).wait_send()
        lev_copy(step).wait_send()
        return carry

    lax.fori_loop(1, num_dev, drain, 0)

    def drain_rows(step, carry):
        for kind in range(0 if low_count == 2 else 1, 2 * high_count if low_count == 2 else high_count):
            if kind != high_count:
                pass_on(rep, source_at(step), kind, step, rep).wait_send()
        return carry

    lax.fori_loop(0, num_dev, drain_rows, 0)
    for part in range(num_rep):
        for kind in range(0 if low_count == 2 else 1, 2 * high_count if low_count == 2 else high_count):
            if kind != high_count:
                white_on(rep, part, kind, rep).wait_send()
    for step in range(1, num_rep):
        lrep_copy(step).wait_send()


def invert_block(block_ref):
    lane = lax.broadcasted_iota(jnp.int32, (PANEL, BLOCK), 1)
    row = lax.broadcasted_iota(jnp.int32, (PANEL, BLOCK), 0)
    lane_all = lax.broadcasted_iota(jnp.int32, (BLOCK, BLOCK), 1)
    for first in range(0, BLOCK, PANEL):
        panel = block_ref[first : first + PANEL, :]
        for at in range(PANEL):
            col = first + at
            column = jnp.broadcast_to(panel[:, col : col + 1], (PANEL, BLOCK))
            inverse_pivot = 1.0 / column[at : at + 1, :]
            pivot_row = jnp.where(lane[:1] == col, 1.0, panel[at : at + 1, :]) * inverse_pivot
            panel = jnp.where(
                row == at, pivot_row, jnp.where(lane == col, 0.0, panel) - column * pivot_row
            )
        whole = block_ref[...]
        inside = (lane_all >= first) & (lane_all < first + PANEL)
        block_ref[...] = jnp.where(inside, 0.0, whole) - dot_full(
            whole[:, first : first + PANEL], panel
        )
        block_ref[first : first + PANEL, :] = panel


def update_kernel(rep_ref, cap_ref, white_ref, inverse_ref, out_ref, cap, block, rows, high, low):
    total = cap.shape[0]

    @pl.when(pl.program_id(0) == 0)
    def _():
        cap[...] = cap_ref[...]

        def eliminate(at, carry):
            where = pl.ds(pl.multiple_of(at * BLOCK, BLOCK), BLOCK)
            block[...] = cap[where, where]
            invert_block(block)
            column = cap[:, where]
            cap[:, where] = jnp.zeros((total, BLOCK), jnp.float32)
            rows[...] = dot_full(block[...], cap[where, :])
            rows[:, where] = block[...]
            cap[...] = cap[...] - dot_full(column, rows[...])
            cap[where, :] = rows[...]
            return carry

        lax.fori_loop(0, total // BLOCK, eliminate, 0)
        solved = dot3(
            two_terms(white_ref[rep_ref[0]]), two_terms(cap[...]), ((0,), (0,))
        )
        high_part, low_part = two_terms(solved)
        high[...] = high_part
        low[...] = low_part

    out_ref[0] = inverse_ref[0] - dot3(
        (high[...], low[...]), two_terms(white_ref[pl.program_id(0)]), ((1,), (0,))
    )


def body(activations, out_grads, inverse):
    num_dev = lax.axis_size("dev")
    num_rep = lax.axis_size("rep")
    examples = activations.shape[1]
    tokens = activations.shape[2]
    feat_width = KI * KO
    group_rows = examples * num_dev
    total = group_rows * num_rep
    width = feat_width // num_rep
    acts_four = activations.reshape(examples, tokens, num_dev, KI)
    grads_four = out_grads.reshape(examples, tokens, num_dev, KO)
    features = jnp.einsum(
        "etmo,etmi->emoi", grads_four, acts_four, preferred_element_type=jnp.float32
    )
    features = features.reshape(examples, num_dev, feat_width) * tokens ** (-0.5)
    to_send = features.transpose(1, 0, 2)
    vmem = pl.BlockSpec(memory_space=pltpu.VMEM)
    hbm = pl.BlockSpec(memory_space=pl.ANY)
    dma = pltpu.SemaphoreType.DMA
    all_white, capacitance, all_lev = pl.pallas_call(
        functools.partial(gather_kernel, num_dev, num_rep, examples),
        name="gather_and_whiten",
        out_shape=(
            jax.ShapeDtypeStruct((num_rep, total, width), jnp.float32),
            jax.ShapeDtypeStruct((total, total), jnp.float32),
            jax.ShapeDtypeStruct((8, total), jnp.float32),
        ),
        in_specs=[vmem, hbm],
        out_specs=(vmem, vmem, vmem),
        scratch_shapes=[
            pltpu.VMEM((total, feat_width), jnp.float32),
            pltpu.VMEM((feat_width, width), jnp.float32),
            pltpu.VMEM((feat_width, width), jnp.bfloat16),
            pltpu.VMEM((feat_width, width), jnp.bfloat16),
            pltpu.VMEM((num_dev, 8, total), jnp.float32),
            pltpu.VMEM((num_rep, 8, total), jnp.float32),
            dma,
            dma,
            dma((num_dev,)),
            dma((num_dev,)),
            dma((num_rep + 1, num_dev)),
            dma((num_rep + 1, num_dev)),
            dma((num_rep + 1, num_rep)),
            dma((num_rep + 1, num_rep)),
            dma((num_dev,)),
            dma((num_dev,)),
            dma((num_rep,)),
            dma((num_rep,)),
        ],
        compiler_params=pltpu.CompilerParams(
            collective_id=0, has_side_effects=True, vmem_limit_bytes=VMEM_BYTES
        ),
    )(to_send, inverse)

    rep = lax.axis_index("rep")
    first_group = rep * group_rows
    own_white = lax.dynamic_slice_in_dim(all_white, first_group, group_rows, 1)
    own_white = own_white.reshape(num_rep, num_dev, examples, width)
    own_white = own_white.transpose(1, 2, 0, 3).reshape(num_dev, examples, 1, feat_width)
    returned = lax.all_to_all(own_white, "dev", split_axis=0, concat_axis=2, tiled=True)
    whitened_out = returned.reshape(1, examples, num_dev * feat_width)

    updated = pl.pallas_call(
        update_kernel,
        name="solve_and_update",
        grid_spec=pltpu.PrefetchScalarGridSpec(
            num_scalar_prefetch=1,
            grid=(num_rep,),
            in_specs=[
                pl.BlockSpec((total, total), lambda c, r: (0, 0)),
                pl.BlockSpec((num_rep, total, width), lambda c, r: (0, 0, 0)),
                pl.BlockSpec((1, width, width), lambda c, r: (0, r[0], c)),
            ],
            out_specs=pl.BlockSpec((1, width, width), lambda c, r: (0, 0, c)),
            scratch_shapes=[
                pltpu.VMEM((total, total), jnp.float32),
                pltpu.VMEM((BLOCK, BLOCK), jnp.float32),
                pltpu.VMEM((BLOCK, total), jnp.float32),
                pltpu.VMEM((width, total), jnp.bfloat16),
                pltpu.VMEM((width, total), jnp.bfloat16),
            ],
        ),
        out_shape=jax.ShapeDtypeStruct((1, width, feat_width), jnp.float32),
        compiler_params=pltpu.CompilerParams(vmem_limit_bytes=VMEM_BYTES),
        cost_estimate=pl.CostEstimate(
            flops=8 * total * width * feat_width, bytes_accessed=16 * total * feat_width, transcendentals=0
        ),
    )(jnp.reshape(rep, (1,)).astype(jnp.int32), capacitance, all_white, inverse)

    lev_first = first_group + lax.axis_index("dev") * examples
    lev_out = lax.dynamic_slice_in_dim(all_lev[0], lev_first, examples, 0).reshape(1, examples)
    return (whitened_out, lev_out, updated)


def solution(mesh):
    in_specs = (P("rep", "dev", None, None), P("rep", "dev", None, None), P("dev", None, None))
    out_specs = (P("rep", "dev", None), P("rep", "dev"), P("dev", "rep", None))
    return jax.shard_map(body, mesh=mesh, in_specs=in_specs, out_specs=out_specs, check_vma=False)
```

```python
import functools

import jax
import jax.numpy as jnp
from jax import lax
from jax.experimental import pallas as pl
from jax.experimental.pallas import tpu as pltpu
from jax.sharding import PartitionSpec as P

KI = 64
KO = 32
VMEM_BYTES = 58 * 1024 * 1024
BLOCK = 128
PANEL = 32
ROWS = 8


def two_terms(value):
    high = value.astype(jnp.bfloat16)
    low = (value - high.astype(jnp.float32)).astype(jnp.bfloat16)
    return high, low


def dot3(left, right, dims):
    left_high, left_low = left
    right_high, right_low = right
    dot = functools.partial(
        lax.dot_general,
        dimension_numbers=(dims, ((), ())),
        preferred_element_type=jnp.float32,
    )
    return dot(left_high, right_high) + (dot(left_high, right_low) + dot(left_low, right_high))


def dot_terms(left, right):
    return dot3(two_terms(left), two_terms(right), ((1,), (0,)))


def gather_kernel(
    num_dev,
    num_rep,
    examples,
    send_ref,
    inverse_ref,
    white_ref,
    high_ref,
    low_ref,
    lev_ref,
    back_ref,
    rows,
    columns,
    cols_high,
    cols_low,
    lev_dev,
    lev_rep,
    partial,
    landed,
    cap,
    work,
    block,
    block_rows,
    load_sem,
    own_sem,
    a2a_send,
    a2a_recv,
    row_send,
    row_recv,
    white_send,
    white_recv,
    lev_send,
    lev_recv,
    lrep_send,
    lrep_recv,
    sum_send,
    sum_recv,
    share_send,
    share_recv,
    back_send,
    back_recv,
    back_own,
):
    dev = lax.axis_index("dev")
    rep = lax.axis_index("rep")
    group = num_dev * examples
    total = num_rep * group
    width = columns.shape[1]
    low_count = 2 if num_rep % 2 == 0 else 1
    high_count = num_rep // low_count
    low = lax.rem(rep, low_count)
    high = rep // low_count
    sibling = high * low_count + (low_count - 1 - low)

    def high_peer(step):
        return lax.rem(high + step, high_count) * low_count + low

    def high_source(step):
        return lax.rem(high + high_count - step, high_count) * low_count + low

    load = pltpu.make_async_copy(
        inverse_ref.at[0, :, pl.ds(pl.multiple_of(rep * width, 128), width)], columns, load_sem
    )
    load.start()

    barrier = pltpu.get_barrier_semaphore()
    for step in range(1, num_dev):
        pl.semaphore_signal(
            barrier, inc=1, device_id={"dev": lax.rem(dev + step, num_dev), "rep": rep}
        )
    for step in range(1, num_rep):
        pl.semaphore_signal(
            barrier, inc=1, device_id={"dev": dev, "rep": lax.rem(rep + step, num_rep)}
        )
    pl.semaphore_wait(barrier, num_dev - 1 + num_rep - 1)

    def row_slice(owner_rep, source):
        return rows.at[pl.ds(pl.multiple_of(owner_rep * group + source * examples, 8), examples)]

    def a2a(step):
        target = lax.rem(dev + step, num_dev)
        return pltpu.make_async_remote_copy(
            src_ref=send_ref.at[target],
            dst_ref=row_slice(rep, dev),
            send_sem=a2a_send.at[step],
            recv_sem=a2a_recv.at[step],
            device_id={"dev": target, "rep": rep},
        )

    own = pltpu.make_async_copy(send_ref.at[dev], row_slice(rep, dev), own_sem)
    own.start()

    def start_a2a(step, carry):
        a2a(step).start()
        return carry

    lax.fori_loop(1, num_dev, start_a2a, 0)

    def pass_on(owner, source, kind, slot, target):
        piece = row_slice(owner, source)
        return pltpu.make_async_remote_copy(
            src_ref=piece,
            dst_ref=piece,
            send_sem=row_send.at[kind, slot],
            recv_sem=row_recv.at[kind, slot],
            device_id={"dev": dev, "rep": target},
        )

    def source_at(step):
        return lax.rem(dev + num_dev - step, num_dev)

    def send_on(step):
        source = source_at(step)
        for far in range(1, high_count):
            pass_on(rep, source, far, step, high_peer(far)).start()
        if low_count == 2:
            pass_on(rep, source, 0, step, sibling).start()

    own.wait()
    send_on(0)
    load.wait()
    high_part, low_part = two_terms(columns[...])
    cols_high[...] = high_part
    cols_low[...] = low_part

    def on_arrival(step, carry):
        a2a(step).wait_recv()
        send_on(step)
        return carry

    lax.fori_loop(1, num_dev, on_arrival, 0)

    def forward(step, carry):
        for far in range(1, high_count):
            pass_on(high_source(far), source_at(step), far, step, rep).wait_recv()
            if low_count == 2:
                pass_on(
                    high_source(far), source_at(step), high_count + far, step, sibling
                ).start()
        return carry

    lax.fori_loop(0, num_dev, forward, 0)

    def finish(step, carry):
        if low_count == 2:
            pass_on(sibling, source_at(step), 0, step, rep).wait_recv()
            for far in range(1, high_count):
                pass_on(sibling, source_at(step), high_count + far, step, rep).wait_recv()
        return carry

    lax.fori_loop(0, num_dev, finish, 0)

    tile = min(256, total)
    own_white = white_ref.at[rep]

    def white_tile(at, carry):
        where = pl.ds(pl.multiple_of(at * tile, tile), tile)
        own_white[where, :] = dot3(
            two_terms(rows[where, :]), (cols_high[...], cols_low[...]), ((1,), (0,))
        )
        return carry

    lax.fori_loop(0, total // tile, white_tile, 0)

    def white_on(owner, part, kind, target):
        piece = white_ref.at[owner, pl.ds(part * group, group)]
        return pltpu.make_async_remote_copy(
            src_ref=piece,
            dst_ref=piece,
            send_sem=white_send.at[kind, part],
            recv_sem=white_recv.at[kind, part],
            device_id={"dev": dev, "rep": target},
        )

    if low_count == 2:
        for part in range(num_rep):
            white_on(rep, part, 0, sibling).start()

    partial[...] = dot3(
        two_terms(rows[:, pl.ds(pl.multiple_of(rep * width, 128), width)]),
        two_terms(white_ref[rep]),
        ((1,), (1,)),
    )

    def group_rows(ref, owner):
        return ref.at[pl.ds(pl.multiple_of(owner * group, 8), group)]

    def sum_copy(step):
        target = lax.rem(rep + step, num_rep)
        return pltpu.make_async_remote_copy(
            src_ref=group_rows(partial, target),
            dst_ref=landed.at[step],
            send_sem=sum_send.at[step],
            recv_sem=sum_recv.at[step],
            device_id={"dev": dev, "rep": target},
        )

    def share_copy(step):
        piece = group_rows(cap, rep)
        return pltpu.make_async_remote_copy(
            src_ref=piece,
            dst_ref=piece,
            send_sem=share_send.at[step],
            recv_sem=share_recv.at[step],
            device_id={"dev": dev, "rep": lax.rem(rep + step, num_rep)},
        )

    for step in range(1, num_rep):
        sum_copy(step).start()

    diagonal = lax.broadcasted_iota(jnp.int32, (total, total), 0) == lax.broadcasted_iota(
        jnp.int32, (total, total), 1
    )
    own_terms = jnp.sum(jnp.where(diagonal, partial[...], 0.0), axis=0, keepdims=True)
    lev_dev[0] = jnp.broadcast_to(own_terms, (8, total))

    def lev_copy(step):
        return pltpu.make_async_remote_copy(
            src_ref=lev_dev.at[0],
            dst_ref=lev_dev.at[step],
            send_sem=lev_send.at[step],
            recv_sem=lev_recv.at[step],
            device_id={"dev": lax.rem(dev + step, num_dev), "rep": rep},
        )

    def lev_start(step, carry):
        lev_copy(step).start()
        return carry

    lax.fori_loop(1, num_dev, lev_start, 0)

    total_rows = partial[pl.ds(pl.multiple_of(rep * group, 8), group), :]
    for step in range(1, num_rep):
        sum_copy(step).wait_recv()
        total_rows = total_rows + landed[step]
    cap[pl.ds(pl.multiple_of(rep * group, 8), group), :] = total_rows
    for step in range(1, num_rep):
        share_copy(step).start()

    def lev_wait(step, carry):
        lev_copy(step).wait_recv()
        return carry

    lax.fori_loop(1, num_dev, lev_wait, 0)
    lev_rep[0] = jnp.sum(lev_dev[...], axis=0)

    def lrep_copy(step):
        return pltpu.make_async_remote_copy(
            src_ref=lev_rep.at[0],
            dst_ref=lev_rep.at[step],
            send_sem=lrep_send.at[step],
            recv_sem=lrep_recv.at[step],
            device_id={"dev": dev, "rep": lax.rem(rep + step, num_rep)},
        )

    for step in range(1, num_rep):
        lrep_copy(step).start()
    for step in range(1, num_rep):
        lrep_copy(step).wait_recv()
    for step in range(1, num_rep):
        share_copy(step).wait_recv()

    def part_order(target):
        if low_count == 2:
            first = target - lax.rem(target, 2)
            other = first + 1 - lax.rem(target, 2)
            return [target, other] + [
                lax.rem(first + at, num_rep) for at in range(2, num_rep)
            ]
        return [lax.rem(target + at, num_rep) for at in range(num_rep)]

    for far in range(1, high_count):
        for part in part_order(high_peer(far)):
            white_on(rep, part, far, high_peer(far)).start()

    leverage = jnp.sum(lev_rep[...], axis=0) / (num_dev * width * num_rep)
    lev_ref[...] = leverage
    damping = 1.0 + (width * num_rep) * leverage[0:1, :]
    work[...] = cap[...] + jnp.where(diagonal, damping, 0.0)

    def back_copy(column_block, slot, step):
        target = lax.rem(dev + step, num_dev)
        first_row = pl.multiple_of(rep * group + target * examples, 8)
        first_column = pl.multiple_of((dev * num_rep + column_block) * width, 128)
        return pltpu.make_async_remote_copy(
            src_ref=white_ref.at[column_block, pl.ds(first_row, examples)],
            dst_ref=back_ref.at[:, pl.ds(first_column, width)],
            send_sem=back_send.at[slot, step],
            recv_sem=back_recv.at[slot, step],
            device_id={"dev": target, "rep": rep},
        )

    def back_local(column_block, slot):
        first_row = pl.multiple_of(rep * group + dev * examples, 8)
        first_column = pl.multiple_of((dev * num_rep + column_block) * width, 128)
        return pltpu.make_async_copy(
            white_ref.at[column_block, pl.ds(first_row, examples)],
            back_ref.at[:, pl.ds(first_column, width)],
            back_own.at[slot],
        )

    def send_back(column_block, slot):
        def start_back(step, carry):
            back_copy(column_block, slot, step).start()
            return carry

        lax.fori_loop(1, num_dev, start_back, 0)
        back_local(column_block, slot).start()

    blocks = [(rep, 0)]
    send_back(rep, 0)
    if low_count == 2:
        for part in range(num_rep):
            white_on(sibling, part, 0, rep).wait_recv()
        blocks.append((sibling, 1))
        send_back(sibling, 1)

    def pass_white(far, places):
        source = high_source(far)
        order = part_order(rep)
        for place in places:
            white_on(source, order[place], far, rep).wait_recv()
            if low_count == 2:
                white_on(source, order[place], high_count + far, sibling).start()

    early = min(2, num_rep)
    block_count = total // BLOCK
    eliminate_blocks(0, block_count // 2, work, block, block_rows)
    for far in range(1, high_count):
        pass_white(far, range(early))
        blocks.append((high_source(far), low_count * far))
        send_back(high_source(far), low_count * far)
    eliminate_blocks(block_count // 2, block_count, work, block, block_rows)
    for far in range(1, high_count):
        pass_white(far, range(early, num_rep))
    if low_count == 2:
        for far in range(1, high_count):
            source = lax.rem(high + high_count - far, high_count) * 2 + (1 - low)
            for part in range(num_rep):
                white_on(source, part, high_count + far, rep).wait_recv()
            blocks.append((source, 2 * far + 1))
            send_back(source, 2 * far + 1)

    solved = dot3(two_terms(white_ref[rep]), two_terms(work[...]), ((0,), (0,)))
    high_part, low_part = two_terms(solved)
    high_ref[...] = high_part
    low_ref[...] = low_part

    for column_block, slot in blocks:

        def back_wait(step, carry, column_block=column_block, slot=slot):
            back_copy(column_block, slot, step).wait()
            return carry

        lax.fori_loop(1, num_dev, back_wait, 0)
        back_local(column_block, slot).wait()

    def drain(step, carry):
        a2a(step).wait_send()
        lev_copy(step).wait_send()
        return carry

    lax.fori_loop(1, num_dev, drain, 0)

    def drain_rows(step, carry):
        for kind in range(0 if low_count == 2 else 1, 2 * high_count if low_count == 2 else high_count):
            if kind != high_count:
                pass_on(rep, source_at(step), kind, step, rep).wait_send()
        return carry

    lax.fori_loop(0, num_dev, drain_rows, 0)
    for part in range(num_rep):
        for kind in range(0 if low_count == 2 else 1, 2 * high_count if low_count == 2 else high_count):
            if kind != high_count:
                white_on(rep, part, kind, rep).wait_send()
    for step in range(1, num_rep):
        lrep_copy(step).wait_send()
        sum_copy(step).wait_send()
        share_copy(step).wait_send()


def invert_block(block_ref):
    lane = lax.broadcasted_iota(jnp.int32, (ROWS, BLOCK), 1)
    row = lax.broadcasted_iota(jnp.int32, (ROWS, BLOCK), 0)
    lane_all = lax.broadcasted_iota(jnp.int32, (BLOCK, BLOCK), 1)

    def spread(value, col):
        return jnp.broadcast_to(value[:, col : col + 1], (ROWS, BLOCK))

    for first in range(0, BLOCK, PANEL):
        panel = [block_ref[at : at + ROWS, :] for at in range(first, first + PANEL, ROWS)]
        for part in range(PANEL // ROWS):
            start = first + part * ROWS
            pivots = panel[part]
            columns = [spread(pivots, start + at) for at in range(ROWS)]
            others = {
                other: [spread(panel[other], start + at) for at in range(ROWS)]
                for other in range(PANEL // ROWS)
                if other != part
            }
            for at in range(ROWS):
                column = columns[at]
                inverse_pivot = 1.0 / column[at : at + 1, :]
                for later in range(at + 1, ROWS):
                    scaled = columns[later][at : at + 1, :] * inverse_pivot
                    columns[later] = jnp.where(
                        row == at, scaled, columns[later] - column * scaled
                    )
                pivot_row = (
                    jnp.where(lane[:1] == start + at, 1.0, pivots[at : at + 1, :])
                    * inverse_pivot
                )
                pivots = jnp.where(
                    row == at,
                    pivot_row,
                    jnp.where(lane == start + at, 0.0, pivots) - column * pivot_row,
                )
            panel[part] = pivots
            for other, spreads in others.items():
                value = jnp.where((lane >= start) & (lane < start + ROWS), 0.0, panel[other])
                for at in range(ROWS):
                    value = value - spreads[at] * pivots[at : at + 1, :]
                panel[other] = value
        panel = jnp.concatenate(panel, axis=0)
        whole = block_ref[...]
        inside = (lane_all >= first) & (lane_all < first + PANEL)
        block_ref[...] = jnp.where(inside, 0.0, whole) - dot_terms(
            whole[:, first : first + PANEL], panel
        )
        block_ref[first : first + PANEL, :] = panel


def eliminate_blocks(begin, end, cap, block, rows):
    total = cap.shape[0]

    def eliminate(at, carry):
        where = pl.ds(pl.multiple_of(at * BLOCK, BLOCK), BLOCK)
        block[...] = cap[where, where]
        invert_block(block)
        column = cap[:, where]
        cap[:, where] = jnp.zeros((total, BLOCK), jnp.float32)
        rows[...] = dot_terms(block[...], cap[where, :])
        rows[:, where] = block[...]
        cap[...] = cap[...] - dot_terms(column, rows[...])
        cap[where, :] = rows[...]
        return carry

    lax.fori_loop(begin, end, eliminate, 0)


def update_kernel(rep_ref, high_ref, low_ref, white_ref, inverse_ref, out_ref):
    out_ref[0] = inverse_ref[0] - dot3(
        (high_ref[...], low_ref[...]), two_terms(white_ref[0]), ((1,), (0,))
    )


def body(activations, out_grads, inverse):
    num_dev = lax.axis_size("dev")
    num_rep = lax.axis_size("rep")
    examples = activations.shape[1]
    tokens = activations.shape[2]
    feat_width = KI * KO
    group_rows = examples * num_dev
    total = group_rows * num_rep
    width = feat_width // num_rep
    acts_four = activations.reshape(examples, tokens, num_dev, KI)
    grads_four = out_grads.reshape(examples, tokens, num_dev, KO)
    features = jnp.einsum(
        "etmo,etmi->emoi", grads_four, acts_four, preferred_element_type=jnp.float32
    )
    features = features.reshape(examples, num_dev, feat_width) * tokens ** (-0.5)
    to_send = features.transpose(1, 0, 2)
    vmem = pl.BlockSpec(memory_space=pltpu.VMEM)
    hbm = pl.BlockSpec(memory_space=pl.ANY)
    dma = pltpu.SemaphoreType.DMA
    all_white, solved_high, solved_low, all_lev, returned = pl.pallas_call(
        functools.partial(gather_kernel, num_dev, num_rep, examples),
        name="gather_whiten_solve",
        out_shape=(
            jax.ShapeDtypeStruct((num_rep, total, width), jnp.float32),
            jax.ShapeDtypeStruct((width, total), jnp.bfloat16),
            jax.ShapeDtypeStruct((width, total), jnp.bfloat16),
            jax.ShapeDtypeStruct((8, total), jnp.float32),
            jax.ShapeDtypeStruct((examples, num_dev * feat_width), jnp.float32),
        ),
        in_specs=[vmem, hbm],
        out_specs=(vmem, vmem, vmem, vmem, hbm),
        scratch_shapes=[
            pltpu.VMEM((total, feat_width), jnp.float32),
            pltpu.VMEM((feat_width, width), jnp.float32),
            pltpu.VMEM((feat_width, width), jnp.bfloat16),
            pltpu.VMEM((feat_width, width), jnp.bfloat16),
            pltpu.VMEM((num_dev, 8, total), jnp.float32),
            pltpu.VMEM((num_rep, 8, total), jnp.float32),
            pltpu.VMEM((total, total), jnp.float32),
            pltpu.VMEM((num_rep, group_rows, total), jnp.float32),
            pltpu.VMEM((total, total), jnp.float32),
            pltpu.VMEM((total, total), jnp.float32),
            pltpu.VMEM((BLOCK, BLOCK), jnp.float32),
            pltpu.VMEM((BLOCK, total), jnp.float32),
            dma,
            dma,
            dma((num_dev,)),
            dma((num_dev,)),
            dma((num_rep + 1, num_dev)),
            dma((num_rep + 1, num_dev)),
            dma((num_rep + 1, num_rep)),
            dma((num_rep + 1, num_rep)),
            dma((num_dev,)),
            dma((num_dev,)),
            dma((num_rep,)),
            dma((num_rep,)),
            dma((num_rep,)),
            dma((num_rep,)),
            dma((num_rep,)),
            dma((num_rep,)),
            dma((num_rep, num_dev)),
            dma((num_rep, num_dev)),
            dma((num_rep,)),
        ],
        compiler_params=pltpu.CompilerParams(
            collective_id=0, has_side_effects=True, vmem_limit_bytes=VMEM_BYTES
        ),
    )(to_send, inverse)

    rep = lax.axis_index("rep")
    updated = pl.pallas_call(
        update_kernel,
        name="update",
        grid_spec=pltpu.PrefetchScalarGridSpec(
            num_scalar_prefetch=1,
            grid=(num_rep,),
            in_specs=[
                pl.BlockSpec((width, total), lambda c, r: (0, 0)),
                pl.BlockSpec((width, total), lambda c, r: (0, 0)),
                pl.BlockSpec((1, total, width), lambda c, r: (c, 0, 0)),
                pl.BlockSpec((1, width, width), lambda c, r: (0, r[0], c)),
            ],
            out_specs=pl.BlockSpec((1, width, width), lambda c, r: (0, 0, c)),
        ),
        out_shape=jax.ShapeDtypeStruct((1, width, feat_width), jnp.float32),
        compiler_params=pltpu.CompilerParams(vmem_limit_bytes=VMEM_BYTES),
        cost_estimate=pl.CostEstimate(
            flops=6 * total * width * feat_width,
            bytes_accessed=12 * width * feat_width,
            transcendentals=0,
        ),
    )(jnp.reshape(rep, (1,)).astype(jnp.int32), solved_high, solved_low, all_white, inverse)

    lev_first = rep * group_rows + lax.axis_index("dev") * examples
    lev_out = lax.dynamic_slice_in_dim(all_lev[0], lev_first, examples, 0).reshape(1, examples)
    return (returned.reshape(1, examples, num_dev * feat_width), lev_out, updated)


def solution(mesh):
    in_specs = (P("rep", "dev", None, None), P("rep", "dev", None, None), P("dev", None, None))
    out_specs = (P("rep", "dev", None), P("rep", "dev"), P("dev", "rep", None))
    return jax.shard_map(body, mesh=mesh, in_specs=in_specs, out_specs=out_specs, check_vma=False)
```

```python
import functools

import jax
import jax.numpy as jnp
from jax import lax
from jax.experimental import pallas as pl
from jax.experimental.pallas import tpu as pltpu
from jax.sharding import PartitionSpec as P

KI = 64
KO = 32
VMEM_BYTES = 58 * 1024 * 1024
BLOCK = 128
PANEL = 32
ROWS = 8


def two_terms(value):
    high = value.astype(jnp.bfloat16)
    low = (value - high.astype(jnp.float32)).astype(jnp.bfloat16)
    return high, low


def dot3(left, right, dims):
    left_high, left_low = left
    right_high, right_low = right
    dot = functools.partial(
        lax.dot_general,
        dimension_numbers=(dims, ((), ())),
        preferred_element_type=jnp.float32,
    )
    return dot(left_high, right_high) + (dot(left_high, right_low) + dot(left_low, right_high))


def dot_full(left, right, dims=((1,), (0,))):
    return lax.dot_general(
        left,
        right,
        dimension_numbers=(dims, ((), ())),
        precision=lax.Precision.HIGHEST,
        preferred_element_type=jnp.float32,
    )


def gather_kernel(
    num_dev,
    num_rep,
    examples,
    send_ref,
    inverse_ref,
    white_ref,
    high_ref,
    low_ref,
    lev_ref,
    back_ref,
    rows,
    columns,
    cols_high,
    cols_low,
    lev_dev,
    lev_rep,
    partial,
    landed,
    cap,
    work,
    block,
    block_rows,
    spread_ref,
    row_ref,
    load_sem,
    own_sem,
    a2a_send,
    a2a_recv,
    row_send,
    row_recv,
    white_send,
    white_recv,
    lev_send,
    lev_recv,
    lrep_send,
    lrep_recv,
    sum_send,
    sum_recv,
    share_send,
    share_recv,
    back_send,
    back_recv,
    back_own,
):
    dev = lax.axis_index("dev")
    rep = lax.axis_index("rep")
    group = num_dev * examples
    total = num_rep * group
    width = columns.shape[1]
    low_count = 2 if num_rep % 2 == 0 else 1
    high_count = num_rep // low_count
    low = lax.rem(rep, low_count)
    high = rep // low_count
    sibling = high * low_count + (low_count - 1 - low)

    def high_peer(step):
        return lax.rem(high + step, high_count) * low_count + low

    def high_source(step):
        return lax.rem(high + high_count - step, high_count) * low_count + low

    load = pltpu.make_async_copy(
        inverse_ref.at[0, :, pl.ds(pl.multiple_of(rep * width, 128), width)], columns, load_sem
    )
    load.start()

    barrier = pltpu.get_barrier_semaphore()
    for step in range(1, num_dev):
        pl.semaphore_signal(
            barrier, inc=1, device_id={"dev": lax.rem(dev + step, num_dev), "rep": rep}
        )
    for step in range(1, num_rep):
        pl.semaphore_signal(
            barrier, inc=1, device_id={"dev": dev, "rep": lax.rem(rep + step, num_rep)}
        )
    pl.semaphore_wait(barrier, num_dev - 1 + num_rep - 1)

    def row_slice(owner_rep, source):
        return rows.at[pl.ds(pl.multiple_of(owner_rep * group + source * examples, 8), examples)]

    def a2a(step):
        target = lax.rem(dev + step, num_dev)
        return pltpu.make_async_remote_copy(
            src_ref=send_ref.at[target],
            dst_ref=row_slice(rep, dev),
            send_sem=a2a_send.at[step],
            recv_sem=a2a_recv.at[step],
            device_id={"dev": target, "rep": rep},
        )

    own = pltpu.make_async_copy(send_ref.at[dev], row_slice(rep, dev), own_sem)
    own.start()

    def start_a2a(step, carry):
        a2a(step).start()
        return carry

    lax.fori_loop(1, num_dev, start_a2a, 0)

    def pass_on(owner, source, kind, slot, target):
        piece = row_slice(owner, source)
        return pltpu.make_async_remote_copy(
            src_ref=piece,
            dst_ref=piece,
            send_sem=row_send.at[kind, slot],
            recv_sem=row_recv.at[kind, slot],
            device_id={"dev": dev, "rep": target},
        )

    def source_at(step):
        return lax.rem(dev + num_dev - step, num_dev)

    def send_on(step):
        source = source_at(step)
        for far in range(1, high_count):
            pass_on(rep, source, far, step, high_peer(far)).start()
        if low_count == 2:
            pass_on(rep, source, 0, step, sibling).start()

    own.wait()
    send_on(0)
    load.wait()
    high_part, low_part = two_terms(columns[...])
    cols_high[...] = high_part
    cols_low[...] = low_part

    def on_arrival(step, carry):
        a2a(step).wait_recv()
        send_on(step)
        return carry

    lax.fori_loop(1, num_dev, on_arrival, 0)

    def forward(step, carry):
        for far in range(1, high_count):
            pass_on(high_source(far), source_at(step), far, step, rep).wait_recv()
            if low_count == 2:
                pass_on(
                    high_source(far), source_at(step), high_count + far, step, sibling
                ).start()
        return carry

    lax.fori_loop(0, num_dev, forward, 0)

    def finish(step, carry):
        if low_count == 2:
            pass_on(sibling, source_at(step), 0, step, rep).wait_recv()
            for far in range(1, high_count):
                pass_on(sibling, source_at(step), high_count + far, step, rep).wait_recv()
        return carry

    lax.fori_loop(0, num_dev, finish, 0)

    tile = min(256, total)
    own_white = white_ref.at[rep]

    def white_tile(at, carry):
        where = pl.ds(pl.multiple_of(at * tile, tile), tile)
        own_white[where, :] = dot3(
            two_terms(rows[where, :]), (cols_high[...], cols_low[...]), ((1,), (0,))
        )
        return carry

    lax.fori_loop(0, total // tile, white_tile, 0)

    def white_on(owner, part, kind, target):
        piece = white_ref.at[owner, pl.ds(part * group, group)]
        return pltpu.make_async_remote_copy(
            src_ref=piece,
            dst_ref=piece,
            send_sem=white_send.at[kind, part],
            recv_sem=white_recv.at[kind, part],
            device_id={"dev": dev, "rep": target},
        )

    def part_order(target):
        if low_count == 2:
            first = target - lax.rem(target, 2)
            other = first + 1 - lax.rem(target, 2)
            return [target, other] + [
                lax.rem(first + at, num_rep) for at in range(2, num_rep)
            ]
        return [lax.rem(target + at, num_rep) for at in range(num_rep)]

    early = min(2, num_rep)

    def send_far(begin, end):
        for far in range(1, high_count):
            for part in part_order(high_peer(far))[begin:end]:
                white_on(rep, part, far, high_peer(far)).start()

    if low_count == 2:
        for part in range(num_rep):
            white_on(rep, part, 0, sibling).start()

    partial[...] = dot3(
        two_terms(rows[:, pl.ds(pl.multiple_of(rep * width, 128), width)]),
        two_terms(white_ref[rep]),
        ((1,), (1,)),
    )

    def group_rows(ref, owner):
        return ref.at[pl.ds(pl.multiple_of(owner * group, 8), group)]

    def sum_copy(step):
        target = lax.rem(rep + step, num_rep)
        return pltpu.make_async_remote_copy(
            src_ref=group_rows(partial, target),
            dst_ref=landed.at[step],
            send_sem=sum_send.at[step],
            recv_sem=sum_recv.at[step],
            device_id={"dev": dev, "rep": target},
        )

    def share_copy(step):
        piece = group_rows(cap, rep)
        return pltpu.make_async_remote_copy(
            src_ref=piece,
            dst_ref=piece,
            send_sem=share_send.at[step],
            recv_sem=share_recv.at[step],
            device_id={"dev": dev, "rep": lax.rem(rep + step, num_rep)},
        )

    for step in range(1, num_rep):
        sum_copy(step).start()
    send_far(0, 1)

    diagonal = lax.broadcasted_iota(jnp.int32, (total, total), 0) == lax.broadcasted_iota(
        jnp.int32, (total, total), 1
    )
    own_terms = jnp.sum(jnp.where(diagonal, partial[...], 0.0), axis=0, keepdims=True)
    lev_dev[0] = jnp.broadcast_to(own_terms, (8, total))

    def lev_copy(step):
        return pltpu.make_async_remote_copy(
            src_ref=lev_dev.at[0],
            dst_ref=lev_dev.at[step],
            send_sem=lev_send.at[step],
            recv_sem=lev_recv.at[step],
            device_id={"dev": lax.rem(dev + step, num_dev), "rep": rep},
        )

    def lev_start(step, carry):
        lev_copy(step).start()
        return carry

    lax.fori_loop(1, num_dev, lev_start, 0)

    total_rows = partial[pl.ds(pl.multiple_of(rep * group, 8), group), :]
    for step in range(1, num_rep):
        sum_copy(step).wait_recv()
        total_rows = total_rows + landed[step]
    cap[pl.ds(pl.multiple_of(rep * group, 8), group), :] = total_rows
    for step in range(1, num_rep):
        share_copy(step).start()
    send_far(1, early)

    def lev_wait(step, carry):
        lev_copy(step).wait_recv()
        return carry

    lax.fori_loop(1, num_dev, lev_wait, 0)
    lev_rep[0] = jnp.sum(lev_dev[...], axis=0)

    def lrep_copy(step):
        return pltpu.make_async_remote_copy(
            src_ref=lev_rep.at[0],
            dst_ref=lev_rep.at[step],
            send_sem=lrep_send.at[step],
            recv_sem=lrep_recv.at[step],
            device_id={"dev": dev, "rep": lax.rem(rep + step, num_rep)},
        )

    for step in range(1, num_rep):
        lrep_copy(step).start()
    for step in range(1, num_rep):
        lrep_copy(step).wait_recv()
    for step in range(1, num_rep):
        share_copy(step).wait_recv()

    send_far(early, num_rep)
    leverage = jnp.sum(lev_rep[...], axis=0) / (num_dev * width * num_rep)
    own_first = rep * group + dev * examples
    lev_ref[...] = pltpu.roll(leverage, total - own_first, 1)[0:1, 0:examples]
    damping = 1.0 + (width * num_rep) * leverage[0:1, :]
    work[...] = cap[...] + jnp.where(diagonal, damping, 0.0)

    def back_copy(column_block, slot, step):
        target = lax.rem(dev + step, num_dev)
        first_row = pl.multiple_of(rep * group + target * examples, 8)
        first_column = pl.multiple_of((dev * num_rep + column_block) * width, 128)
        return pltpu.make_async_remote_copy(
            src_ref=white_ref.at[column_block, pl.ds(first_row, examples)],
            dst_ref=back_ref.at[:, pl.ds(first_column, width)],
            send_sem=back_send.at[slot, step],
            recv_sem=back_recv.at[slot, step],
            device_id={"dev": target, "rep": rep},
        )

    def back_local(column_block, slot):
        first_row = pl.multiple_of(rep * group + dev * examples, 8)
        first_column = pl.multiple_of((dev * num_rep + column_block) * width, 128)
        return pltpu.make_async_copy(
            white_ref.at[column_block, pl.ds(first_row, examples)],
            back_ref.at[:, pl.ds(first_column, width)],
            back_own.at[slot],
        )

    def send_back(column_block, slot):
        def start_back(step, carry):
            back_copy(column_block, slot, step).start()
            return carry

        lax.fori_loop(1, num_dev, start_back, 0)
        back_local(column_block, slot).start()

    blocks = [(rep, 0)]
    send_back(rep, 0)
    if low_count == 2:
        for part in range(num_rep):
            white_on(sibling, part, 0, rep).wait_recv()
        blocks.append((sibling, 1))
        send_back(sibling, 1)

    def pass_white(far, places):
        source = high_source(far)
        order = part_order(rep)
        for place in places:
            white_on(source, order[place], far, rep).wait_recv()
            if low_count == 2:
                white_on(source, order[place], high_count + far, sibling).start()

    block_count = total // BLOCK
    eliminate_blocks(0, block_count // 2, work, block, block_rows, spread_ref, row_ref)
    for far in range(1, high_count):
        pass_white(far, range(early))
        blocks.append((high_source(far), low_count * far))
        send_back(high_source(far), low_count * far)
    eliminate_blocks(block_count // 2, block_count, work, block, block_rows, spread_ref, row_ref)
    for far in range(1, high_count):
        pass_white(far, range(early, num_rep))
    if low_count == 2:
        for far in range(1, high_count):
            source = lax.rem(high + high_count - far, high_count) * 2 + (1 - low)
            for part in range(num_rep):
                white_on(source, part, high_count + far, rep).wait_recv()
            blocks.append((source, 2 * far + 1))
            send_back(source, 2 * far + 1)

    solved = dot_full(white_ref[rep], work[...], ((0,), (0,)))
    high_part, low_part = two_terms(solved)
    high_ref[...] = high_part
    low_ref[...] = low_part

    for column_block, slot in blocks:

        def back_wait(step, carry, column_block=column_block, slot=slot):
            back_copy(column_block, slot, step).wait()
            return carry

        lax.fori_loop(1, num_dev, back_wait, 0)
        back_local(column_block, slot).wait()

    def drain(step, carry):
        a2a(step).wait_send()
        lev_copy(step).wait_send()
        return carry

    lax.fori_loop(1, num_dev, drain, 0)

    def drain_rows(step, carry):
        for kind in range(0 if low_count == 2 else 1, 2 * high_count if low_count == 2 else high_count):
            if kind != high_count:
                pass_on(rep, source_at(step), kind, step, rep).wait_send()
        return carry

    lax.fori_loop(0, num_dev, drain_rows, 0)
    for part in range(num_rep):
        for kind in range(0 if low_count == 2 else 1, 2 * high_count if low_count == 2 else high_count):
            if kind != high_count:
                white_on(rep, part, kind, rep).wait_send()
    for step in range(1, num_rep):
        lrep_copy(step).wait_send()
        sum_copy(step).wait_send()
        share_copy(step).wait_send()


def sweep_pairs(entry):
    def at(i, j):
        return entry[min(i, j), max(i, j)]

    for one in range(0, ROWS, 2):
        two = one + 1
        first, cross, second = at(one, one), at(one, two), at(two, two)
        scale = 1.0 / (first * second - cross * cross)
        p11, p12, p22 = second * scale, cross * scale, first * scale
        rest = [i for i in range(ROWS) if i not in (one, two)]
        scaled = {
            i: (
                at(i, one) * p11 - at(i, two) * p12,
                at(i, two) * p22 - at(i, one) * p12,
            )
            for i in rest
        }
        for i in rest:
            for j in rest:
                if i <= j:
                    entry[i, j] = entry[i, j] - (
                        scaled[i][0] * at(j, one) + scaled[i][1] * at(j, two)
                    )
        for i in rest:
            entry[min(i, one), max(i, one)] = scaled[i][0]
            entry[min(i, two), max(i, two)] = scaled[i][1]
        entry[one, one], entry[one, two], entry[two, two] = -p11, p12, -p22
    return entry


def invert_block(block_ref, spread_ref, row_ref):
    lane = lax.broadcasted_iota(jnp.int32, (ROWS, BLOCK), 1)
    row = lax.broadcasted_iota(jnp.int32, (ROWS, BLOCK), 0)
    lane_all = lax.broadcasted_iota(jnp.int32, (BLOCK, BLOCK), 1)

    def spread(value, col):
        return jnp.broadcast_to(value[:, col : col + 1], (ROWS, BLOCK))

    def whole_row(ref, at):
        return jnp.broadcast_to(ref[at : at + 1, :], (ROWS, BLOCK))

    for first in range(0, BLOCK, PANEL):
        panel = [block_ref[at : at + ROWS, :] for at in range(first, first + PANEL, ROWS)]
        for part in range(PANEL // ROWS):
            start = first + part * ROWS
            inside = (lane >= start) & (lane < start + ROWS)
            for at in range(ROWS):
                spread_ref[at * ROWS : (at + 1) * ROWS, :] = spread(panel[part], start + at)
            row_ref[0:ROWS, :] = jnp.where(
                inside, jnp.where(lane - start == row, 1.0, 0.0), panel[part]
            )
            others = {
                other: [spread(panel[other], start + at) for at in range(ROWS)]
                for other in range(PANEL // ROWS)
                if other != part
            }
            entry = sweep_pairs(
                {
                    (i, j): whole_row(spread_ref, j * ROWS + i)
                    for j in range(ROWS)
                    for i in range(j + 1)
                }
            )
            pivots = None
            for at in range(ROWS):
                column = entry[0, at]
                for i in range(1, ROWS):
                    column = jnp.where(row == i, entry[min(i, at), max(i, at)], column)
                term = column * whole_row(row_ref, at)
                pivots = -term if pivots is None else pivots - term
            panel[part] = pivots
            row_ref[ROWS : 2 * ROWS, :] = pivots
            for other, spreads in others.items():
                value = jnp.where(inside, 0.0, panel[other])
                for at in range(ROWS):
                    value = value - spreads[at] * whole_row(row_ref, ROWS + at)
                panel[other] = value
        panel = jnp.concatenate(panel, axis=0)
        whole = block_ref[...]
        inside = (lane_all >= first) & (lane_all < first + PANEL)
        block_ref[...] = jnp.where(inside, 0.0, whole) - dot_full(
            whole[:, first : first + PANEL], panel
        )
        block_ref[first : first + PANEL, :] = panel


def eliminate_blocks(begin, end, cap, block, rows, spread_ref, row_ref):
    total = cap.shape[0]

    def eliminate(at, carry):
        where = pl.ds(pl.multiple_of(at * BLOCK, BLOCK), BLOCK)
        block[...] = cap[where, where]
        invert_block(block, spread_ref, row_ref)
        column = cap[:, where]
        cap[:, where] = jnp.zeros((total, BLOCK), jnp.float32)
        rows[...] = dot_full(block[...], cap[where, :])
        rows[:, where] = block[...]
        cap[...] = cap[...] - dot_full(column, rows[...])
        cap[where, :] = rows[...]
        return carry

    lax.fori_loop(begin, end, eliminate, 0)


def update_kernel(
    rep_ref, high_ref, low_ref, white_ref, inverse_ref, back_ref, out_ref, whitened_ref
):
    whitened_ref[0] = back_ref[...]
    out_ref[0] = inverse_ref[0] - dot3(
        (high_ref[...], low_ref[...]), two_terms(white_ref[0]), ((1,), (0,))
    )


def body(activations, out_grads, inverse):
    num_dev = lax.axis_size("dev")
    num_rep = lax.axis_size("rep")
    examples = activations.shape[1]
    tokens = activations.shape[2]
    feat_width = KI * KO
    group_rows = examples * num_dev
    total = group_rows * num_rep
    width = feat_width // num_rep
    acts_four = activations.reshape(examples, tokens, num_dev, KI)
    grads_four = out_grads.reshape(examples, tokens, num_dev, KO)
    features = jnp.einsum(
        "etmo,etmi->emoi", grads_four, acts_four, preferred_element_type=jnp.float32
    )
    features = features.reshape(examples, num_dev, feat_width) * tokens ** (-0.5)
    to_send = features.transpose(1, 0, 2)
    vmem = pl.BlockSpec(memory_space=pltpu.VMEM)
    hbm = pl.BlockSpec(memory_space=pl.ANY)
    dma = pltpu.SemaphoreType.DMA
    all_white, solved_high, solved_low, lev_out, returned = pl.pallas_call(
        functools.partial(gather_kernel, num_dev, num_rep, examples),
        name="gather_whiten_solve",
        out_shape=(
            jax.ShapeDtypeStruct((num_rep, total, width), jnp.float32),
            jax.ShapeDtypeStruct((width, total), jnp.bfloat16),
            jax.ShapeDtypeStruct((width, total), jnp.bfloat16),
            jax.ShapeDtypeStruct((1, examples), jnp.float32),
            jax.ShapeDtypeStruct((examples, num_dev * feat_width), jnp.float32),
        ),
        in_specs=[vmem, hbm],
        out_specs=(vmem, vmem, vmem, vmem, hbm),
        scratch_shapes=[
            pltpu.VMEM((total, feat_width), jnp.float32),
            pltpu.VMEM((feat_width, width), jnp.float32),
            pltpu.VMEM((feat_width, width), jnp.bfloat16),
            pltpu.VMEM((feat_width, width), jnp.bfloat16),
            pltpu.VMEM((num_dev, 8, total), jnp.float32),
            pltpu.VMEM((num_rep, 8, total), jnp.float32),
            pltpu.VMEM((total, total), jnp.float32),
            pltpu.VMEM((num_rep, group_rows, total), jnp.float32),
            pltpu.VMEM((total, total), jnp.float32),
            pltpu.VMEM((total, total), jnp.float32),
            pltpu.VMEM((BLOCK, BLOCK), jnp.float32),
            pltpu.VMEM((BLOCK, total), jnp.float32),
            pltpu.VMEM((ROWS * ROWS, BLOCK), jnp.float32),
            pltpu.VMEM((2 * ROWS, BLOCK), jnp.float32),
            dma,
            dma,
            dma((num_dev,)),
            dma((num_dev,)),
            dma((num_rep + 1, num_dev)),
            dma((num_rep + 1, num_dev)),
            dma((num_rep + 1, num_rep)),
            dma((num_rep + 1, num_rep)),
            dma((num_dev,)),
            dma((num_dev,)),
            dma((num_rep,)),
            dma((num_rep,)),
            dma((num_rep,)),
            dma((num_rep,)),
            dma((num_rep,)),
            dma((num_rep,)),
            dma((num_rep, num_dev)),
            dma((num_rep, num_dev)),
            dma((num_rep,)),
        ],
        compiler_params=pltpu.CompilerParams(
            collective_id=0, has_side_effects=True, vmem_limit_bytes=VMEM_BYTES
        ),
    )(to_send, inverse)

    rep = lax.axis_index("rep")
    updated, whitened_out = pl.pallas_call(
        update_kernel,
        name="update",
        grid_spec=pltpu.PrefetchScalarGridSpec(
            num_scalar_prefetch=1,
            grid=(num_rep,),
            in_specs=[
                pl.BlockSpec((width, total), lambda c, r: (0, 0)),
                pl.BlockSpec((width, total), lambda c, r: (0, 0)),
                pl.BlockSpec((1, total, width), lambda c, r: (c, 0, 0)),
                pl.BlockSpec((1, width, width), lambda c, r: (0, r[0], c)),
                pl.BlockSpec((examples, num_dev * width), lambda c, r: (0, c)),
            ],
            out_specs=(
                pl.BlockSpec((1, width, width), lambda c, r: (0, 0, c)),
                pl.BlockSpec((1, examples, num_dev * width), lambda c, r: (0, 0, c)),
            ),
        ),
        out_shape=(
            jax.ShapeDtypeStruct((1, width, feat_width), jnp.float32),
            jax.ShapeDtypeStruct((1, examples, num_dev * feat_width), jnp.float32),
        ),
        compiler_params=pltpu.CompilerParams(vmem_limit_bytes=VMEM_BYTES),
        cost_estimate=pl.CostEstimate(
            flops=6 * total * width * feat_width,
            bytes_accessed=12 * width * feat_width,
            transcendentals=0,
        ),
    )(jnp.reshape(rep, (1,)).astype(jnp.int32), solved_high, solved_low, all_white, inverse, returned)

    return (whitened_out, lev_out, updated)


def solution(mesh):
    in_specs = (P("rep", "dev", None, None), P("rep", "dev", None, None), P("dev", None, None))
    out_specs = (P("rep", "dev", None), P("rep", "dev"), P("dev", "rep", None))
    return jax.shard_map(body, mesh=mesh, in_specs=in_specs, out_specs=out_specs, check_vma=False)
```

```python
import functools

import jax
import jax.numpy as jnp
from jax import lax
from jax.experimental import pallas as pl
from jax.experimental.pallas import tpu as pltpu
from jax.sharding import PartitionSpec as P

KI = 64
KO = 32
VMEM_BYTES = 58 * 1024 * 1024
BLOCK = 128
PANEL = 32
ROWS = 8


def two_terms(value):
    high = value.astype(jnp.bfloat16)
    low = (value - high.astype(jnp.float32)).astype(jnp.bfloat16)
    return high, low


def dot3(left, right, dims):
    left_high, left_low = left
    right_high, right_low = right
    dot = functools.partial(
        lax.dot_general,
        dimension_numbers=(dims, ((), ())),
        preferred_element_type=jnp.float32,
    )
    return dot(left_high, right_high) + (dot(left_high, right_low) + dot(left_low, right_high))


def dot_full(left, right, dims=((1,), (0,))):
    return lax.dot_general(
        left,
        right,
        dimension_numbers=(dims, ((), ())),
        precision=lax.Precision.HIGHEST,
        preferred_element_type=jnp.float32,
    )


def gather_kernel(
    num_dev,
    num_rep,
    examples,
    send_ref,
    inverse_ref,
    white_ref,
    high_ref,
    low_ref,
    lev_ref,
    back_ref,
    rows,
    columns,
    cols_high,
    cols_low,
    lev_dev,
    lev_rep,
    partial,
    landed,
    cap,
    work,
    block,
    block_rows,
    spread_ref,
    row_ref,
    load_sem,
    own_sem,
    a2a_send,
    a2a_recv,
    row_send,
    row_recv,
    white_send,
    white_recv,
    lev_send,
    lev_recv,
    lrep_send,
    lrep_recv,
    sum_send,
    sum_recv,
    share_send,
    share_recv,
    back_send,
    back_recv,
    back_own,
):
    dev = lax.axis_index("dev")
    rep = lax.axis_index("rep")
    group = num_dev * examples
    total = num_rep * group
    width = columns.shape[1]
    low_count = 2 if num_rep % 2 == 0 else 1
    high_count = num_rep // low_count
    low = lax.rem(rep, low_count)
    high = rep // low_count
    sibling = high * low_count + (low_count - 1 - low)

    def high_peer(step):
        return lax.rem(high + step, high_count) * low_count + low

    def high_source(step):
        return lax.rem(high + high_count - step, high_count) * low_count + low

    load = pltpu.make_async_copy(
        inverse_ref.at[0, :, pl.ds(pl.multiple_of(rep * width, 128), width)], columns, load_sem
    )
    load.start()

    barrier = pltpu.get_barrier_semaphore()
    for step in range(1, num_dev):
        pl.semaphore_signal(
            barrier, inc=1, device_id={"dev": lax.rem(dev + step, num_dev), "rep": rep}
        )
    for step in range(1, num_rep):
        pl.semaphore_signal(
            barrier, inc=1, device_id={"dev": dev, "rep": lax.rem(rep + step, num_rep)}
        )
    pl.semaphore_wait(barrier, num_dev - 1 + num_rep - 1)

    def row_slice(owner_rep, source):
        return rows.at[pl.ds(pl.multiple_of(owner_rep * group + source * examples, 8), examples)]

    def a2a(step):
        target = lax.rem(dev + step, num_dev)
        return pltpu.make_async_remote_copy(
            src_ref=send_ref.at[target],
            dst_ref=row_slice(rep, dev),
            send_sem=a2a_send.at[step],
            recv_sem=a2a_recv.at[step],
            device_id={"dev": target, "rep": rep},
        )

    own = pltpu.make_async_copy(send_ref.at[dev], row_slice(rep, dev), own_sem)
    own.start()

    def start_a2a(step, carry):
        a2a(step).start()
        return carry

    lax.fori_loop(1, num_dev, start_a2a, 0)

    def pass_on(owner, source, kind, slot, target):
        piece = row_slice(owner, source)
        return pltpu.make_async_remote_copy(
            src_ref=piece,
            dst_ref=piece,
            send_sem=row_send.at[kind, slot],
            recv_sem=row_recv.at[kind, slot],
            device_id={"dev": dev, "rep": target},
        )

    def source_at(step):
        return lax.rem(dev + num_dev - step, num_dev)

    def send_on(step):
        source = source_at(step)
        for far in range(1, high_count):
            pass_on(rep, source, far, step, high_peer(far)).start()
        if low_count == 2:
            pass_on(rep, source, 0, step, sibling).start()

    own.wait()
    send_on(0)
    load.wait()
    high_part, low_part = two_terms(columns[...])
    cols_high[...] = high_part
    cols_low[...] = low_part

    def on_arrival(step, carry):
        a2a(step).wait_recv()
        send_on(step)
        return carry

    lax.fori_loop(1, num_dev, on_arrival, 0)

    def forward(step, carry):
        for far in range(1, high_count):
            pass_on(high_source(far), source_at(step), far, step, rep).wait_recv()
            if low_count == 2:
                pass_on(
                    high_source(far), source_at(step), high_count + far, step, sibling
                ).start()
        return carry

    lax.fori_loop(0, num_dev, forward, 0)

    def finish(step, carry):
        if low_count == 2:
            pass_on(sibling, source_at(step), 0, step, rep).wait_recv()
            for far in range(1, high_count):
                pass_on(sibling, source_at(step), high_count + far, step, rep).wait_recv()
        return carry

    lax.fori_loop(0, num_dev, finish, 0)

    tile = min(256, total)
    own_white = white_ref.at[rep]

    def white_tile(at, carry):
        where = pl.ds(pl.multiple_of(at * tile, tile), tile)
        own_white[where, :] = dot3(
            two_terms(rows[where, :]), (cols_high[...], cols_low[...]), ((1,), (0,))
        )
        return carry

    lax.fori_loop(0, total // tile, white_tile, 0)

    def white_on(owner, part, kind, target):
        piece = white_ref.at[owner, pl.ds(part * group, group)]
        return pltpu.make_async_remote_copy(
            src_ref=piece,
            dst_ref=piece,
            send_sem=white_send.at[kind, part],
            recv_sem=white_recv.at[kind, part],
            device_id={"dev": dev, "rep": target},
        )

    def part_order(target):
        if low_count == 2:
            first = target - lax.rem(target, 2)
            other = first + 1 - lax.rem(target, 2)
            return [target, other] + [
                lax.rem(first + at, num_rep) for at in range(2, num_rep)
            ]
        return [lax.rem(target + at, num_rep) for at in range(num_rep)]

    early = min(2, num_rep)

    def send_far(begin, end):
        for far in range(1, high_count):
            for part in part_order(high_peer(far))[begin:end]:
                white_on(rep, part, far, high_peer(far)).start()

    if low_count == 2:
        for part in range(num_rep):
            white_on(rep, part, 0, sibling).start()

    partial[...] = dot3(
        two_terms(rows[:, pl.ds(pl.multiple_of(rep * width, 128), width)]),
        two_terms(white_ref[rep]),
        ((1,), (1,)),
    )

    def group_rows(ref, owner):
        return ref.at[pl.ds(pl.multiple_of(owner * group, 8), group)]

    def sum_copy(step):
        target = lax.rem(rep + step, num_rep)
        return pltpu.make_async_remote_copy(
            src_ref=group_rows(partial, target),
            dst_ref=landed.at[step],
            send_sem=sum_send.at[step],
            recv_sem=sum_recv.at[step],
            device_id={"dev": dev, "rep": target},
        )

    def share_copy(step):
        piece = group_rows(cap, rep)
        return pltpu.make_async_remote_copy(
            src_ref=piece,
            dst_ref=piece,
            send_sem=share_send.at[step],
            recv_sem=share_recv.at[step],
            device_id={"dev": dev, "rep": lax.rem(rep + step, num_rep)},
        )

    for step in range(1, num_rep):
        sum_copy(step).start()

    diagonal = lax.broadcasted_iota(jnp.int32, (total, total), 0) == lax.broadcasted_iota(
        jnp.int32, (total, total), 1
    )
    own_terms = jnp.sum(jnp.where(diagonal, partial[...], 0.0), axis=0, keepdims=True)
    lev_dev[0] = jnp.broadcast_to(own_terms, (8, total))

    def lev_copy(step):
        return pltpu.make_async_remote_copy(
            src_ref=lev_dev.at[0],
            dst_ref=lev_dev.at[step],
            send_sem=lev_send.at[step],
            recv_sem=lev_recv.at[step],
            device_id={"dev": lax.rem(dev + step, num_dev), "rep": rep},
        )

    def lev_start(step, carry):
        lev_copy(step).start()
        return carry

    lax.fori_loop(1, num_dev, lev_start, 0)

    total_rows = partial[pl.ds(pl.multiple_of(rep * group, 8), group), :]
    for step in range(1, num_rep):
        sum_copy(step).wait_recv()
        total_rows = total_rows + landed[step]
    cap[pl.ds(pl.multiple_of(rep * group, 8), group), :] = total_rows
    for step in range(1, num_rep):
        share_copy(step).start()

    def lev_wait(step, carry):
        lev_copy(step).wait_recv()
        return carry

    lax.fori_loop(1, num_dev, lev_wait, 0)
    lev_rep[0] = jnp.sum(lev_dev[...], axis=0)

    def lrep_copy(step):
        return pltpu.make_async_remote_copy(
            src_ref=lev_rep.at[0],
            dst_ref=lev_rep.at[step],
            send_sem=lrep_send.at[step],
            recv_sem=lrep_recv.at[step],
            device_id={"dev": dev, "rep": lax.rem(rep + step, num_rep)},
        )

    for step in range(1, num_rep):
        lrep_copy(step).start()
    for step in range(1, num_rep):
        lrep_copy(step).wait_recv()
    for step in range(1, num_rep):
        share_copy(step).wait_recv()

    send_far(0, num_rep)
    leverage = jnp.sum(lev_rep[...], axis=0) / (num_dev * width * num_rep)
    own_first = rep * group + dev * examples
    lev_ref[...] = pltpu.roll(leverage, total - own_first, 1)[0:1, 0:examples]
    damping = 1.0 + (width * num_rep) * leverage[0:1, :]
    work[...] = cap[...] + jnp.where(diagonal, damping, 0.0)

    def back_copy(column_block, slot, step):
        target = lax.rem(dev + step, num_dev)
        first_row = pl.multiple_of(rep * group + target * examples, 8)
        first_column = pl.multiple_of((dev * num_rep + column_block) * width, 128)
        return pltpu.make_async_remote_copy(
            src_ref=white_ref.at[column_block, pl.ds(first_row, examples)],
            dst_ref=back_ref.at[:, pl.ds(first_column, width)],
            send_sem=back_send.at[slot, step],
            recv_sem=back_recv.at[slot, step],
            device_id={"dev": target, "rep": rep},
        )

    def back_local(column_block, slot):
        first_row = pl.multiple_of(rep * group + dev * examples, 8)
        first_column = pl.multiple_of((dev * num_rep + column_block) * width, 128)
        return pltpu.make_async_copy(
            white_ref.at[column_block, pl.ds(first_row, examples)],
            back_ref.at[:, pl.ds(first_column, width)],
            back_own.at[slot],
        )

    def send_back(column_block, slot):
        def start_back(step, carry):
            back_copy(column_block, slot, step).start()
            return carry

        lax.fori_loop(1, num_dev, start_back, 0)
        back_local(column_block, slot).start()

    blocks = [(rep, 0)]
    send_back(rep, 0)
    if low_count == 2:
        for part in range(num_rep):
            white_on(sibling, part, 0, rep).wait_recv()
        blocks.append((sibling, 1))
        send_back(sibling, 1)

    def pass_white(far, places):
        source = high_source(far)
        order = part_order(rep)
        for place in places:
            white_on(source, order[place], far, rep).wait_recv()
            if low_count == 2:
                white_on(source, order[place], high_count + far, sibling).start()

    block_count = total // BLOCK
    eliminate_blocks(0, block_count // 2, work, block, block_rows, spread_ref, row_ref)
    for far in range(1, high_count):
        pass_white(far, range(early))
        blocks.append((high_source(far), low_count * far))
        send_back(high_source(far), low_count * far)
    eliminate_blocks(block_count // 2, block_count, work, block, block_rows, spread_ref, row_ref)
    for far in range(1, high_count):
        pass_white(far, range(early, num_rep))
    if low_count == 2:
        for far in range(1, high_count):
            source = lax.rem(high + high_count - far, high_count) * 2 + (1 - low)
            for part in range(num_rep):
                white_on(source, part, high_count + far, rep).wait_recv()
            blocks.append((source, 2 * far + 1))
            send_back(source, 2 * far + 1)

    solved = dot_full(white_ref[rep], work[...], ((0,), (0,)))
    high_part, low_part = two_terms(solved)
    high_ref[...] = high_part
    low_ref[...] = low_part

    for column_block, slot in blocks:

        def back_wait(step, carry, column_block=column_block, slot=slot):
            back_copy(column_block, slot, step).wait()
            return carry

        lax.fori_loop(1, num_dev, back_wait, 0)
        back_local(column_block, slot).wait()

    def drain(step, carry):
        a2a(step).wait_send()
        lev_copy(step).wait_send()
        return carry

    lax.fori_loop(1, num_dev, drain, 0)

    def drain_rows(step, carry):
        for kind in range(0 if low_count == 2 else 1, 2 * high_count if low_count == 2 else high_count):
            if kind != high_count:
                pass_on(rep, source_at(step), kind, step, rep).wait_send()
        return carry

    lax.fori_loop(0, num_dev, drain_rows, 0)
    for part in range(num_rep):
        for kind in range(0 if low_count == 2 else 1, 2 * high_count if low_count == 2 else high_count):
            if kind != high_count:
                white_on(rep, part, kind, rep).wait_send()
    for step in range(1, num_rep):
        lrep_copy(step).wait_send()
        sum_copy(step).wait_send()
        share_copy(step).wait_send()


def sweep_pairs(entry):
    def at(i, j):
        return entry[min(i, j), max(i, j)]

    for one in range(0, ROWS, 2):
        two = one + 1
        first, cross, second = at(one, one), at(one, two), at(two, two)
        scale = 1.0 / (first * second - cross * cross)
        p11, p12, p22 = second * scale, cross * scale, first * scale
        rest = [i for i in range(ROWS) if i not in (one, two)]
        scaled = {
            i: (
                at(i, one) * p11 - at(i, two) * p12,
                at(i, two) * p22 - at(i, one) * p12,
            )
            for i in rest
        }
        for i in rest:
            for j in rest:
                if i <= j:
                    entry[i, j] = entry[i, j] - (
                        scaled[i][0] * at(j, one) + scaled[i][1] * at(j, two)
                    )
        for i in rest:
            entry[min(i, one), max(i, one)] = scaled[i][0]
            entry[min(i, two), max(i, two)] = scaled[i][1]
        entry[one, one], entry[one, two], entry[two, two] = -p11, p12, -p22
    return entry


def invert_block(block_ref, spread_ref, row_ref):
    lane = lax.broadcasted_iota(jnp.int32, (ROWS, BLOCK), 1)
    row = lax.broadcasted_iota(jnp.int32, (ROWS, BLOCK), 0)
    lane_all = lax.broadcasted_iota(jnp.int32, (BLOCK, BLOCK), 1)

    def spread(value, col):
        return jnp.broadcast_to(value[:, col : col + 1], (ROWS, BLOCK))

    def whole_row(ref, at):
        return jnp.broadcast_to(ref[at : at + 1, :], (ROWS, BLOCK))

    for first in range(0, BLOCK, PANEL):
        panel = [block_ref[at : at + ROWS, :] for at in range(first, first + PANEL, ROWS)]
        for part in range(PANEL // ROWS):
            start = first + part * ROWS
            inside = (lane >= start) & (lane < start + ROWS)
            for at in range(ROWS):
                spread_ref[at * ROWS : (at + 1) * ROWS, :] = spread(panel[part], start + at)
            row_ref[0:ROWS, :] = jnp.where(
                inside, jnp.where(lane - start == row, 1.0, 0.0), panel[part]
            )
            others = {
                other: [spread(panel[other], start + at) for at in range(ROWS)]
                for other in range(PANEL // ROWS)
                if other != part
            }
            entry = sweep_pairs(
                {
                    (i, j): whole_row(spread_ref, j * ROWS + i)
                    for j in range(ROWS)
                    for i in range(j + 1)
                }
            )
            pivots = None
            for at in range(ROWS):
                column = entry[0, at]
                for i in range(1, ROWS):
                    column = jnp.where(row == i, entry[min(i, at), max(i, at)], column)
                term = column * whole_row(row_ref, at)
                pivots = -term if pivots is None else pivots - term
            panel[part] = pivots
            row_ref[ROWS : 2 * ROWS, :] = pivots
            for other, spreads in others.items():
                value = jnp.where(inside, 0.0, panel[other])
                for at in range(ROWS):
                    value = value - spreads[at] * whole_row(row_ref, ROWS + at)
                panel[other] = value
        panel = jnp.concatenate(panel, axis=0)
        whole = block_ref[...]
        inside = (lane_all >= first) & (lane_all < first + PANEL)
        block_ref[...] = jnp.where(inside, 0.0, whole) - dot_full(
            whole[:, first : first + PANEL], panel
        )
        block_ref[first : first + PANEL, :] = panel


def eliminate_blocks(begin, end, cap, block, rows, spread_ref, row_ref):
    total = cap.shape[0]

    def eliminate(at, carry):
        where = pl.ds(pl.multiple_of(at * BLOCK, BLOCK), BLOCK)
        block[...] = cap[where, where]
        invert_block(block, spread_ref, row_ref)
        column = cap[:, where]
        cap[:, where] = jnp.zeros((total, BLOCK), jnp.float32)
        rows[...] = dot_full(block[...], cap[where, :])
        rows[:, where] = block[...]
        cap[...] = cap[...] - dot_full(column, rows[...])
        cap[where, :] = rows[...]
        return carry

    lax.fori_loop(begin, end, eliminate, 0)


def update_kernel(
    rep_ref, high_ref, low_ref, white_ref, inverse_ref, back_ref, out_ref, whitened_ref
):
    whitened_ref[0] = back_ref[...]
    out_ref[0] = inverse_ref[0] - dot3(
        (high_ref[...], low_ref[...]), two_terms(white_ref[0]), ((1,), (0,))
    )


def body(activations, out_grads, inverse):
    num_dev = lax.axis_size("dev")
    num_rep = lax.axis_size("rep")
    examples = activations.shape[1]
    tokens = activations.shape[2]
    feat_width = KI * KO
    group_rows = examples * num_dev
    total = group_rows * num_rep
    width = feat_width // num_rep
    acts_four = activations.reshape(examples, tokens, num_dev, KI)
    grads_four = out_grads.reshape(examples, tokens, num_dev, KO)
    features = jnp.einsum(
        "etmo,etmi->meoi", grads_four, acts_four, preferred_element_type=jnp.float32
    )
    to_send = features.reshape(num_dev, examples, feat_width) * tokens ** (-0.5)
    vmem = pl.BlockSpec(memory_space=pltpu.VMEM)
    hbm = pl.BlockSpec(memory_space=pl.ANY)
    dma = pltpu.SemaphoreType.DMA
    all_white, solved_high, solved_low, lev_out, returned = pl.pallas_call(
        functools.partial(gather_kernel, num_dev, num_rep, examples),
        name="gather_whiten_solve",
        out_shape=(
            jax.ShapeDtypeStruct((num_rep, total, width), jnp.float32),
            jax.ShapeDtypeStruct((width, total), jnp.bfloat16),
            jax.ShapeDtypeStruct((width, total), jnp.bfloat16),
            jax.ShapeDtypeStruct((1, examples), jnp.float32),
            jax.ShapeDtypeStruct((examples, num_dev * feat_width), jnp.float32),
        ),
        in_specs=[vmem, hbm],
        out_specs=(vmem, vmem, vmem, vmem, hbm),
        scratch_shapes=[
            pltpu.VMEM((total, feat_width), jnp.float32),
            pltpu.VMEM((feat_width, width), jnp.float32),
            pltpu.VMEM((feat_width, width), jnp.bfloat16),
            pltpu.VMEM((feat_width, width), jnp.bfloat16),
            pltpu.VMEM((num_dev, 8, total), jnp.float32),
            pltpu.VMEM((num_rep, 8, total), jnp.float32),
            pltpu.VMEM((total, total), jnp.float32),
            pltpu.VMEM((num_rep, group_rows, total), jnp.float32),
            pltpu.VMEM((total, total), jnp.float32),
            pltpu.VMEM((total, total), jnp.float32),
            pltpu.VMEM((BLOCK, BLOCK), jnp.float32),
            pltpu.VMEM((BLOCK, total), jnp.float32),
            pltpu.VMEM((ROWS * ROWS, BLOCK), jnp.float32),
            pltpu.VMEM((2 * ROWS, BLOCK), jnp.float32),
            dma,
            dma,
            dma((num_dev,)),
            dma((num_dev,)),
            dma((num_rep + 1, num_dev)),
            dma((num_rep + 1, num_dev)),
            dma((num_rep + 1, num_rep)),
            dma((num_rep + 1, num_rep)),
            dma((num_dev,)),
            dma((num_dev,)),
            dma((num_rep,)),
            dma((num_rep,)),
            dma((num_rep,)),
            dma((num_rep,)),
            dma((num_rep,)),
            dma((num_rep,)),
            dma((num_rep, num_dev)),
            dma((num_rep, num_dev)),
            dma((num_rep,)),
        ],
        compiler_params=pltpu.CompilerParams(
            collective_id=0, has_side_effects=True, vmem_limit_bytes=VMEM_BYTES
        ),
    )(to_send, inverse)

    rep = lax.axis_index("rep")
    updated, whitened_out = pl.pallas_call(
        update_kernel,
        name="update",
        grid_spec=pltpu.PrefetchScalarGridSpec(
            num_scalar_prefetch=1,
            grid=(num_rep,),
            in_specs=[
                pl.BlockSpec((width, total), lambda c, r: (0, 0)),
                pl.BlockSpec((width, total), lambda c, r: (0, 0)),
                pl.BlockSpec((1, total, width), lambda c, r: (c, 0, 0)),
                pl.BlockSpec((1, width, width), lambda c, r: (0, r[0], c)),
                pl.BlockSpec((examples, num_dev * width), lambda c, r: (0, c)),
            ],
            out_specs=(
                pl.BlockSpec((1, width, width), lambda c, r: (0, 0, c)),
                pl.BlockSpec((1, examples, num_dev * width), lambda c, r: (0, 0, c)),
            ),
        ),
        out_shape=(
            jax.ShapeDtypeStruct((1, width, feat_width), jnp.float32),
            jax.ShapeDtypeStruct((1, examples, num_dev * feat_width), jnp.float32),
        ),
        compiler_params=pltpu.CompilerParams(vmem_limit_bytes=VMEM_BYTES),
        cost_estimate=pl.CostEstimate(
            flops=6 * total * width * feat_width,
            bytes_accessed=12 * width * feat_width,
            transcendentals=0,
        ),
    )(jnp.reshape(rep, (1,)).astype(jnp.int32), solved_high, solved_low, all_white, inverse, returned)

    return (whitened_out, lev_out, updated)


def solution(mesh):
    in_specs = (P("rep", "dev", None, None), P("rep", "dev", None, None), P("dev", None, None))
    out_specs = (P("rep", "dev", None), P("rep", "dev"), P("dev", "rep", None))
    return jax.shard_map(body, mesh=mesh, in_specs=in_specs, out_specs=out_specs, check_vma=False)
```

```python
import functools

import jax
import jax.numpy as jnp
from jax import lax
from jax.experimental import pallas as pl
from jax.experimental.pallas import tpu as pltpu
from jax.sharding import PartitionSpec as P

KI = 64
KO = 32
VMEM_BYTES = 58 * 1024 * 1024
BLOCK = 128
PANEL = 32
ROWS = 8


def two_terms(value):
    high = value.astype(jnp.bfloat16)
    low = (value - high.astype(jnp.float32)).astype(jnp.bfloat16)
    return high, low


def dot3(left, right, dims):
    left_high, left_low = left
    right_high, right_low = right
    dot = functools.partial(
        lax.dot_general,
        dimension_numbers=(dims, ((), ())),
        preferred_element_type=jnp.float32,
    )
    return dot(left_high, right_high) + (dot(left_high, right_low) + dot(left_low, right_high))


def dot_full(left, right, dims=((1,), (0,))):
    return lax.dot_general(
        left,
        right,
        dimension_numbers=(dims, ((), ())),
        precision=lax.Precision.HIGHEST,
        preferred_element_type=jnp.float32,
    )


def gather_kernel(
    num_dev,
    num_rep,
    examples,
    send_ref,
    inverse_ref,
    white_ref,
    high_ref,
    low_ref,
    lev_ref,
    back_ref,
    rows,
    columns,
    cols_high,
    cols_low,
    lev_dev,
    lev_rep,
    partial,
    landed,
    cap,
    work,
    block,
    block_rows,
    spread_ref,
    row_ref,
    load_sem,
    own_sem,
    a2a_send,
    a2a_recv,
    row_send,
    row_recv,
    white_send,
    white_recv,
    lev_send,
    lev_recv,
    lrep_send,
    lrep_recv,
    sum_send,
    sum_recv,
    share_send,
    share_recv,
    back_send,
    back_recv,
    back_own,
):
    dev = lax.axis_index("dev")
    rep = lax.axis_index("rep")
    group = num_dev * examples
    total = num_rep * group
    width = columns.shape[1]
    low_count = 2 if num_rep % 2 == 0 else 1
    high_count = num_rep // low_count
    low = lax.rem(rep, low_count)
    high = rep // low_count
    sibling = high * low_count + (low_count - 1 - low)

    def high_peer(step):
        return lax.rem(high + step, high_count) * low_count + low

    def high_source(step):
        return lax.rem(high + high_count - step, high_count) * low_count + low

    load = pltpu.make_async_copy(
        inverse_ref.at[0, :, pl.ds(pl.multiple_of(rep * width, 128), width)], columns, load_sem
    )
    load.start()

    barrier = pltpu.get_barrier_semaphore()
    for step in range(1, num_dev):
        pl.semaphore_signal(
            barrier, inc=1, device_id={"dev": lax.rem(dev + step, num_dev), "rep": rep}
        )
    for step in range(1, num_rep):
        pl.semaphore_signal(
            barrier, inc=1, device_id={"dev": dev, "rep": lax.rem(rep + step, num_rep)}
        )
    pl.semaphore_wait(barrier, num_dev - 1 + num_rep - 1)

    def row_slice(owner_rep, source):
        return rows.at[pl.ds(pl.multiple_of(owner_rep * group + source * examples, 8), examples)]

    def a2a(step):
        target = lax.rem(dev + step, num_dev)
        return pltpu.make_async_remote_copy(
            src_ref=send_ref.at[target],
            dst_ref=row_slice(rep, dev),
            send_sem=a2a_send.at[step],
            recv_sem=a2a_recv.at[step],
            device_id={"dev": target, "rep": rep},
        )

    own = pltpu.make_async_copy(send_ref.at[dev], row_slice(rep, dev), own_sem)
    own.start()

    def start_a2a(step, carry):
        a2a(step).start()
        return carry

    lax.fori_loop(1, num_dev, start_a2a, 0)

    def pass_on(owner, source, kind, slot, target):
        piece = row_slice(owner, source)
        return pltpu.make_async_remote_copy(
            src_ref=piece,
            dst_ref=piece,
            send_sem=row_send.at[kind, slot],
            recv_sem=row_recv.at[kind, slot],
            device_id={"dev": dev, "rep": target},
        )

    def source_at(step):
        return lax.rem(dev + num_dev - step, num_dev)

    def send_on(step):
        source = source_at(step)
        for far in range(1, high_count):
            pass_on(rep, source, far, step, high_peer(far)).start()
        if low_count == 2:
            pass_on(rep, source, 0, step, sibling).start()

    own.wait()
    send_on(0)
    load.wait()
    high_part, low_part = two_terms(columns[...])
    cols_high[...] = high_part
    cols_low[...] = low_part

    def on_arrival(step, carry):
        a2a(step).wait_recv()
        send_on(step)
        return carry

    lax.fori_loop(1, num_dev, on_arrival, 0)

    def forward(step, carry):
        for far in range(1, high_count):
            pass_on(high_source(far), source_at(step), far, step, rep).wait_recv()
            if low_count == 2:
                pass_on(
                    high_source(far), source_at(step), high_count + far, step, sibling
                ).start()
        return carry

    lax.fori_loop(0, num_dev, forward, 0)

    def finish(step, carry):
        if low_count == 2:
            pass_on(sibling, source_at(step), 0, step, rep).wait_recv()
            for far in range(1, high_count):
                pass_on(sibling, source_at(step), high_count + far, step, rep).wait_recv()
        return carry

    lax.fori_loop(0, num_dev, finish, 0)

    tile = min(256, total)
    own_white = white_ref.at[rep]

    def white_tile(at, carry):
        where = pl.ds(pl.multiple_of(at * tile, tile), tile)
        own_white[where, :] = dot3(
            two_terms(rows[where, :]), (cols_high[...], cols_low[...]), ((1,), (0,))
        )
        return carry

    lax.fori_loop(0, total // tile, white_tile, 0)

    def white_on(owner, part, kind, target):
        piece = white_ref.at[owner, pl.ds(part * group, group)]
        return pltpu.make_async_remote_copy(
            src_ref=piece,
            dst_ref=piece,
            send_sem=white_send.at[kind, part],
            recv_sem=white_recv.at[kind, part],
            device_id={"dev": dev, "rep": target},
        )

    def part_order(target):
        if low_count == 2:
            first = target - lax.rem(target, 2)
            other = first + 1 - lax.rem(target, 2)
            return [target, other] + [
                lax.rem(first + at, num_rep) for at in range(2, num_rep)
            ]
        return [lax.rem(target + at, num_rep) for at in range(num_rep)]

    early = min(2, num_rep)

    def send_far(begin, end):
        for far in range(1, high_count):
            for part in part_order(high_peer(far))[begin:end]:
                white_on(rep, part, far, high_peer(far)).start()

    if low_count == 2:
        for part in range(num_rep):
            white_on(rep, part, 0, sibling).start()

    partial[...] = dot3(
        two_terms(rows[:, pl.ds(pl.multiple_of(rep * width, 128), width)]),
        two_terms(white_ref[rep]),
        ((1,), (1,)),
    )

    def group_rows(ref, owner):
        return ref.at[pl.ds(pl.multiple_of(owner * group, 8), group)]

    def sum_copy(step):
        target = lax.rem(rep + step, num_rep)
        return pltpu.make_async_remote_copy(
            src_ref=group_rows(partial, target),
            dst_ref=landed.at[step],
            send_sem=sum_send.at[step],
            recv_sem=sum_recv.at[step],
            device_id={"dev": dev, "rep": target},
        )

    def share_copy(step):
        piece = group_rows(cap, rep)
        return pltpu.make_async_remote_copy(
            src_ref=piece,
            dst_ref=piece,
            send_sem=share_send.at[step],
            recv_sem=share_recv.at[step],
            device_id={"dev": dev, "rep": lax.rem(rep + step, num_rep)},
        )

    for step in range(1, num_rep):
        sum_copy(step).start()

    diagonal = lax.broadcasted_iota(jnp.int32, (total, total), 0) == lax.broadcasted_iota(
        jnp.int32, (total, total), 1
    )
    own_terms = jnp.sum(jnp.where(diagonal, partial[...], 0.0), axis=0, keepdims=True)
    lev_dev[0] = jnp.broadcast_to(own_terms, (8, total))

    def lev_copy(step):
        return pltpu.make_async_remote_copy(
            src_ref=lev_dev.at[0],
            dst_ref=lev_dev.at[step],
            send_sem=lev_send.at[step],
            recv_sem=lev_recv.at[step],
            device_id={"dev": lax.rem(dev + step, num_dev), "rep": rep},
        )

    def lev_start(step, carry):
        lev_copy(step).start()
        return carry

    lax.fori_loop(1, num_dev, lev_start, 0)

    total_rows = partial[pl.ds(pl.multiple_of(rep * group, 8), group), :]
    for step in range(1, num_rep):
        sum_copy(step).wait_recv()
        total_rows = total_rows + landed[step]
    cap[pl.ds(pl.multiple_of(rep * group, 8), group), :] = total_rows
    for step in range(1, num_rep):
        share_copy(step).start()

    def lev_wait(step, carry):
        lev_copy(step).wait_recv()
        return carry

    lax.fori_loop(1, num_dev, lev_wait, 0)
    lev_rep[0] = jnp.sum(lev_dev[...], axis=0)

    def lrep_copy(step):
        return pltpu.make_async_remote_copy(
            src_ref=lev_rep.at[0],
            dst_ref=lev_rep.at[step],
            send_sem=lrep_send.at[step],
            recv_sem=lrep_recv.at[step],
            device_id={"dev": dev, "rep": lax.rem(rep + step, num_rep)},
        )

    for step in range(1, num_rep):
        lrep_copy(step).start()
    for step in range(1, num_rep):
        lrep_copy(step).wait_recv()
    for step in range(1, num_rep):
        share_copy(step).wait_recv()

    send_far(0, num_rep)
    leverage = jnp.sum(lev_rep[...], axis=0) / (num_dev * width * num_rep)
    own_first = rep * group + dev * examples
    lev_ref[...] = pltpu.roll(leverage, total - own_first, 1)[0:1, 0:examples]
    damping = 1.0 + (width * num_rep) * leverage[0:1, :]
    work[...] = cap[...] + jnp.where(diagonal, damping, 0.0)

    def back_copy(column_block, slot, step):
        target = lax.rem(dev + step, num_dev)
        first_row = pl.multiple_of(rep * group + target * examples, 8)
        first_column = pl.multiple_of((dev * num_rep + column_block) * width, 128)
        return pltpu.make_async_remote_copy(
            src_ref=white_ref.at[column_block, pl.ds(first_row, examples)],
            dst_ref=back_ref.at[:, pl.ds(first_column, width)],
            send_sem=back_send.at[slot, step],
            recv_sem=back_recv.at[slot, step],
            device_id={"dev": target, "rep": rep},
        )

    def back_local(column_block, slot):
        first_row = pl.multiple_of(rep * group + dev * examples, 8)
        first_column = pl.multiple_of((dev * num_rep + column_block) * width, 128)
        return pltpu.make_async_copy(
            white_ref.at[column_block, pl.ds(first_row, examples)],
            back_ref.at[:, pl.ds(first_column, width)],
            back_own.at[slot],
        )

    def send_back(column_block, slot):
        def start_back(step, carry):
            back_copy(column_block, slot, step).start()
            return carry

        lax.fori_loop(1, num_dev, start_back, 0)
        back_local(column_block, slot).start()

    blocks = [(rep, 0)]
    send_back(rep, 0)
    if low_count == 2:
        for part in range(num_rep):
            white_on(sibling, part, 0, rep).wait_recv()
        blocks.append((sibling, 1))
        send_back(sibling, 1)

    def pass_white(far, places):
        source = high_source(far)
        order = part_order(rep)
        for place in places:
            white_on(source, order[place], far, rep).wait_recv()
            if low_count == 2:
                white_on(source, order[place], high_count + far, sibling).start()

    block_count = total // BLOCK
    eliminate_blocks(0, block_count // 2, work, block, block_rows, spread_ref, row_ref)
    for far in range(1, high_count):
        pass_white(far, range(early))
        blocks.append((high_source(far), low_count * far))
        send_back(high_source(far), low_count * far)
    eliminate_blocks(block_count // 2, block_count, work, block, block_rows, spread_ref, row_ref)
    last = []
    if low_count == 2:
        for far in range(1, high_count):
            source = lax.rem(high + high_count - far, high_count) * 2 + (1 - low)
            white_on(source, rep, high_count + far, rep).wait_recv()
            blocks.append((source, 2 * far + 1))
            send_back(source, 2 * far + 1)
            last.append((source, high_count + far))
    for far in range(1, high_count):
        pass_white(far, range(early, num_rep))

    solved = dot_full(white_ref[rep], work[...], ((0,), (0,)))
    high_part, low_part = two_terms(solved)
    high_ref[...] = high_part
    low_ref[...] = low_part

    for source, kind in last:
        for at in range(1, num_rep):
            white_on(source, lax.rem(rep + at, num_rep), kind, rep).wait_recv()

    for column_block, slot in blocks:

        def back_wait(step, carry, column_block=column_block, slot=slot):
            back_copy(column_block, slot, step).wait()
            return carry

        lax.fori_loop(1, num_dev, back_wait, 0)
        back_local(column_block, slot).wait()

    def drain(step, carry):
        a2a(step).wait_send()
        lev_copy(step).wait_send()
        return carry

    lax.fori_loop(1, num_dev, drain, 0)

    def drain_rows(step, carry):
        for kind in range(0 if low_count == 2 else 1, 2 * high_count if low_count == 2 else high_count):
            if kind != high_count:
                pass_on(rep, source_at(step), kind, step, rep).wait_send()
        return carry

    lax.fori_loop(0, num_dev, drain_rows, 0)
    for part in range(num_rep):
        for kind in range(0 if low_count == 2 else 1, 2 * high_count if low_count == 2 else high_count):
            if kind != high_count:
                white_on(rep, part, kind, rep).wait_send()
    for step in range(1, num_rep):
        lrep_copy(step).wait_send()
        sum_copy(step).wait_send()
        share_copy(step).wait_send()


def sweep_pairs(entry):
    def at(i, j):
        return entry[min(i, j), max(i, j)]

    for one in range(0, ROWS, 2):
        two = one + 1
        first, cross, second = at(one, one), at(one, two), at(two, two)
        scale = 1.0 / (first * second - cross * cross)
        p11, p12, p22 = second * scale, cross * scale, first * scale
        rest = [i for i in range(ROWS) if i not in (one, two)]
        scaled = {
            i: (
                at(i, one) * p11 - at(i, two) * p12,
                at(i, two) * p22 - at(i, one) * p12,
            )
            for i in rest
        }
        for i in rest:
            for j in rest:
                if i <= j:
                    entry[i, j] = entry[i, j] - (
                        scaled[i][0] * at(j, one) + scaled[i][1] * at(j, two)
                    )
        for i in rest:
            entry[min(i, one), max(i, one)] = scaled[i][0]
            entry[min(i, two), max(i, two)] = scaled[i][1]
        entry[one, one], entry[one, two], entry[two, two] = -p11, p12, -p22
    return entry


def invert_block(block_ref, spread_ref, row_ref):
    lane = lax.broadcasted_iota(jnp.int32, (ROWS, BLOCK), 1)
    row = lax.broadcasted_iota(jnp.int32, (ROWS, BLOCK), 0)
    lane_all = lax.broadcasted_iota(jnp.int32, (BLOCK, BLOCK), 1)

    def spread(value, col):
        return jnp.broadcast_to(value[:, col : col + 1], (ROWS, BLOCK))

    def whole_row(ref, at):
        return jnp.broadcast_to(ref[at : at + 1, :], (ROWS, BLOCK))

    for first in range(0, BLOCK, PANEL):
        panel = [block_ref[at : at + ROWS, :] for at in range(first, first + PANEL, ROWS)]
        for part in range(PANEL // ROWS):
            start = first + part * ROWS
            inside = (lane >= start) & (lane < start + ROWS)
            for at in range(ROWS):
                spread_ref[at * ROWS : (at + 1) * ROWS, :] = spread(panel[part], start + at)
            row_ref[0:ROWS, :] = jnp.where(
                inside, jnp.where(lane - start == row, 1.0, 0.0), panel[part]
            )
            others = {
                other: [spread(panel[other], start + at) for at in range(ROWS)]
                for other in range(PANEL // ROWS)
                if other != part
            }
            entry = sweep_pairs(
                {
                    (i, j): whole_row(spread_ref, j * ROWS + i)
                    for j in range(ROWS)
                    for i in range(j + 1)
                }
            )
            pivots = None
            for at in range(ROWS):
                column = entry[0, at]
                for i in range(1, ROWS):
                    column = jnp.where(row == i, entry[min(i, at), max(i, at)], column)
                term = column * whole_row(row_ref, at)
                pivots = -term if pivots is None else pivots - term
            panel[part] = pivots
            row_ref[ROWS : 2 * ROWS, :] = pivots
            for other, spreads in others.items():
                value = jnp.where(inside, 0.0, panel[other])
                for at in range(ROWS):
                    value = value - spreads[at] * whole_row(row_ref, ROWS + at)
                panel[other] = value
        panel = jnp.concatenate(panel, axis=0)
        whole = block_ref[...]
        inside = (lane_all >= first) & (lane_all < first + PANEL)
        block_ref[...] = jnp.where(inside, 0.0, whole) - dot_full(
            whole[:, first : first + PANEL], panel
        )
        block_ref[first : first + PANEL, :] = panel


def eliminate_blocks(begin, end, cap, block, rows, spread_ref, row_ref):
    total = cap.shape[0]

    def eliminate(at, carry):
        where = pl.ds(pl.multiple_of(at * BLOCK, BLOCK), BLOCK)
        block[...] = cap[where, where]
        invert_block(block, spread_ref, row_ref)
        column = cap[:, where]
        cap[:, where] = jnp.zeros((total, BLOCK), jnp.float32)
        rows[...] = dot_full(block[...], cap[where, :])
        rows[:, where] = block[...]
        cap[...] = cap[...] - dot_full(column, rows[...])
        cap[where, :] = rows[...]
        return carry

    lax.fori_loop(begin, end, eliminate, 0)


def update_kernel(
    rep_ref, high_ref, low_ref, white_ref, inverse_ref, back_ref, out_ref, whitened_ref
):
    whitened_ref[0] = back_ref[...]
    out_ref[0] = inverse_ref[0] - dot3(
        (high_ref[...], low_ref[...]), two_terms(white_ref[0]), ((1,), (0,))
    )


def body(activations, out_grads, inverse):
    num_dev = lax.axis_size("dev")
    num_rep = lax.axis_size("rep")
    examples = activations.shape[1]
    tokens = activations.shape[2]
    feat_width = KI * KO
    group_rows = examples * num_dev
    total = group_rows * num_rep
    width = feat_width // num_rep
    acts_four = activations.reshape(examples, tokens, num_dev, KI)
    grads_four = out_grads.reshape(examples, tokens, num_dev, KO)
    features = jnp.einsum(
        "etmo,etmi->meoi", grads_four, acts_four, preferred_element_type=jnp.float32
    )
    to_send = features.reshape(num_dev, examples, feat_width) * tokens ** (-0.5)
    vmem = pl.BlockSpec(memory_space=pltpu.VMEM)
    hbm = pl.BlockSpec(memory_space=pl.ANY)
    dma = pltpu.SemaphoreType.DMA
    all_white, solved_high, solved_low, lev_out, returned = pl.pallas_call(
        functools.partial(gather_kernel, num_dev, num_rep, examples),
        name="gather_whiten_solve",
        out_shape=(
            jax.ShapeDtypeStruct((num_rep, total, width), jnp.float32),
            jax.ShapeDtypeStruct((width, total), jnp.bfloat16),
            jax.ShapeDtypeStruct((width, total), jnp.bfloat16),
            jax.ShapeDtypeStruct((1, examples), jnp.float32),
            jax.ShapeDtypeStruct((examples, num_dev * feat_width), jnp.float32),
        ),
        in_specs=[vmem, hbm],
        out_specs=(vmem, vmem, vmem, vmem, hbm),
        scratch_shapes=[
            pltpu.VMEM((total, feat_width), jnp.float32),
            pltpu.VMEM((feat_width, width), jnp.float32),
            pltpu.VMEM((feat_width, width), jnp.bfloat16),
            pltpu.VMEM((feat_width, width), jnp.bfloat16),
            pltpu.VMEM((num_dev, 8, total), jnp.float32),
            pltpu.VMEM((num_rep, 8, total), jnp.float32),
            pltpu.VMEM((total, total), jnp.float32),
            pltpu.VMEM((num_rep, group_rows, total), jnp.float32),
            pltpu.VMEM((total, total), jnp.float32),
            pltpu.VMEM((total, total), jnp.float32),
            pltpu.VMEM((BLOCK, BLOCK), jnp.float32),
            pltpu.VMEM((BLOCK, total), jnp.float32),
            pltpu.VMEM((ROWS * ROWS, BLOCK), jnp.float32),
            pltpu.VMEM((2 * ROWS, BLOCK), jnp.float32),
            dma,
            dma,
            dma((num_dev,)),
            dma((num_dev,)),
            dma((num_rep + 1, num_dev)),
            dma((num_rep + 1, num_dev)),
            dma((num_rep + 1, num_rep)),
            dma((num_rep + 1, num_rep)),
            dma((num_dev,)),
            dma((num_dev,)),
            dma((num_rep,)),
            dma((num_rep,)),
            dma((num_rep,)),
            dma((num_rep,)),
            dma((num_rep,)),
            dma((num_rep,)),
            dma((num_rep, num_dev)),
            dma((num_rep, num_dev)),
            dma((num_rep,)),
        ],
        compiler_params=pltpu.CompilerParams(
            collective_id=0, has_side_effects=True, vmem_limit_bytes=VMEM_BYTES
        ),
    )(to_send, inverse)

    rep = lax.axis_index("rep")
    updated, whitened_out = pl.pallas_call(
        update_kernel,
        name="update",
        grid_spec=pltpu.PrefetchScalarGridSpec(
            num_scalar_prefetch=1,
            grid=(num_rep,),
            in_specs=[
                pl.BlockSpec((width, total), lambda c, r: (0, 0)),
                pl.BlockSpec((width, total), lambda c, r: (0, 0)),
                pl.BlockSpec((1, total, width), lambda c, r: (c, 0, 0)),
                pl.BlockSpec((1, width, width), lambda c, r: (0, r[0], c)),
                pl.BlockSpec((examples, num_dev * width), lambda c, r: (0, c)),
            ],
            out_specs=(
                pl.BlockSpec((1, width, width), lambda c, r: (0, 0, c)),
                pl.BlockSpec((1, examples, num_dev * width), lambda c, r: (0, 0, c)),
            ),
        ),
        out_shape=(
            jax.ShapeDtypeStruct((1, width, feat_width), jnp.float32),
            jax.ShapeDtypeStruct((1, examples, num_dev * feat_width), jnp.float32),
        ),
        compiler_params=pltpu.CompilerParams(vmem_limit_bytes=VMEM_BYTES),
        cost_estimate=pl.CostEstimate(
            flops=6 * total * width * feat_width,
            bytes_accessed=12 * width * feat_width,
            transcendentals=0,
        ),
    )(jnp.reshape(rep, (1,)).astype(jnp.int32), solved_high, solved_low, all_white, inverse, returned)

    return (whitened_out, lev_out, updated)


def solution(mesh):
    in_specs = (P("rep", "dev", None, None), P("rep", "dev", None, None), P("dev", None, None))
    out_specs = (P("rep", "dev", None), P("rep", "dev"), P("dev", "rep", None))
    return jax.shard_map(body, mesh=mesh, in_specs=in_specs, out_specs=out_specs, check_vma=False)
```
